32 devices in a mesh: dom: 8 (over z, x), rel: 4 (over y, core).
Axes of the slice: x: 2, y: 2, z: 4, core: 2. Of those that a mesh axis runs over, the one named last changes fastest.
Arguments:
- emb: float32 [2048, 400], P('dom'), may hold values from -1.2 to 1.2
- emb_state: float32 [2048], P('dom'), may hold values from 0.02 to 2
- rel_weight: float32 [32, 400], P('rel'), may hold values from 0.5 to 1.5
- rel_state: float32 [32], P('rel'), may hold values from 1 to 1000
- swap_mask: int32 [1], replicated, may hold values from 1 to 7
- src_rows: int32 [4, 4096], P('rel', 'dom'), may hold values from 0 to 255
- dst_rows: int32 [4, 4096], P('rel', 'dom'), may hold values from 0 to 255
- tile_rel: int32 [4, 32], P('rel', 'dom'), may hold values from 0 to 7
- live_tiles: int32 [4, 8], P('rel', 'dom'), may hold values from 1 to 4, as said below
- neg_tiles: int32 [4, 64], P('rel', 'dom'), may hold values from 0 to 1
- bound_rows: int32 [2048], P('dom'), may hold values from 0 to 255
- band_src: int32 [4, 2048], P('rel', 'dom'), may hold values from 0 to 255
- band_dst: int32 [4, 2048], P('rel', 'dom'), may hold values from 0 to 255
- band_rel: int32 [4, 16], P('rel', 'dom'), may hold values from 0 to 7
Outputs:
- emb_new: float32 [2048, 400], P('dom')
- state_new: float32 [2048], P('dom')
- rel_new: float32 [32, 400], P('rel')
The draws below stay inside these ranges and needn't reach their ends.
Inputs may be any that keep to these rules, and one draw needn't show every extreme that they name: `live_tiles`: each entry counts the leading edge tiles of one bucket that hold edges; some relation group and partition has all 4 tiles live in every draw. `swap_mask`: the same plan entry holds for every partition, so pairs are mutual.
All inputs are finite; a program needn't handle non-finite values.
Results may differ from the reference program's by a relative error of at most 0.0029.
Values may be sent and summed in bfloat16 or wider, within the bound.
A program may use at most 64 MiB of HBM per device.

```python
import math
import jax
import jax.numpy as jnp
from jax import lax

D = 400
TILE = 128
P_ROWS = 256
E_TILES = 4
BAND_TILES = 2
NEG_TILES = 8
BND = 128
RELS_DEV = 8
ENT = 2048
RELS = 32
E_ROWS = 512
BAND_ROWS = 256
NEG = 1024
P_TILES = 2
N_DOM = 8
N_REL = 4


def draw_live_tiles(key, part):
    base = jax.random.fold_in(key, 11)
    first, second = jax.random.split(base)
    counts = jax.random.randint(first, (N_REL * N_DOM,), 1, E_TILES + 1)
    place = jax.random.randint(second, (), 0, N_REL * N_DOM)
    counts = jnp.where(jnp.arange(N_REL * N_DOM) == place, E_TILES, counts)
    return counts.reshape(N_REL, N_DOM).astype(jnp.int32)


def draw_rel_state(key, part):
    base = jax.random.fold_in(key, 23)
    values = jnp.exp(jax.random.uniform(base, (RELS,), jnp.float32, 0.0, 6.9))
    return values.astype(jnp.float32)


def set_ends(values, own_key, smallest, largest):
    spot = [jax.random.randint(jax.random.fold_in(own_key, axis), (), 0, length) for axis, length in enumerate(values.shape)]
    longest = values.shape.index(max(values.shape))
    beside = spot[:longest] + [(spot[longest] + 1) % values.shape[longest]] + spot[longest + 1:]
    return values.at[tuple(spot)].set(smallest).at[tuple(beside)].set(largest)


def level_of(rng, dims, cuts, low, top_value):
    gain, own = 1.0, jax.random.fold_in(rng, 6)
    for position, shards_of in cuts:
        draws = jnp.exp(jax.random.uniform(jax.random.fold_in(own, position), (shards_of,), jnp.float32, low / len(cuts), top_value / len(cuts)))
        gain = gain * jnp.repeat(draws, dims[position] // shards_of).reshape([-1 if axis == position else 1 for axis in range(len(dims))])
    return gain


def scatter_about(key, shape, scale, reach, cuts=(), dtype=jnp.bfloat16):
    factor_of = level_of(key, shape, cuts, -0.22, 0.18) if cuts else 1.0
    result = jax.random.normal(key, shape, jnp.float32) * scale * factor_of
    return jnp.minimum(jnp.maximum(result, -reach), reach).astype(dtype)


def setup_inputs(seed: int = 0) -> dict:
    streams_of = jax.random.split(jax.random.key(seed), 15)
    return {
        "emb": scatter_about(streams_of[0], (ENT, D), 0.2, 1.2, ((0, 8),), jnp.float32),
        "emb_state": jnp.clip(jnp.exp(math.log(2.0) - 4.6051702 * jax.random.uniform(streams_of[1], (ENT,), jnp.float32) ** level_of(streams_of[1], (ENT,), ((0, 8),), -0.2, 0.2)), 0.02, 2.0),
        "rel_weight": jnp.clip(1.0 + 0.1 * jax.random.normal(streams_of[2], (RELS, D), jnp.float32), 0.5, 1.5),
        "rel_state": draw_rel_state(jax.random.fold_in(streams_of[14], 71), 0),
        "swap_mask": jax.random.randint(streams_of[4], (1,), 1, N_DOM).astype(jnp.int32),
        "src_rows": set_ends(jax.random.randint(streams_of[5], (N_REL, N_DOM * E_ROWS), 0, P_ROWS), jax.random.fold_in(streams_of[5], 1), 0, P_ROWS - 1).astype(jnp.int32),
        "dst_rows": set_ends(jax.random.randint(streams_of[6], (N_REL, N_DOM * E_ROWS), 0, P_ROWS), jax.random.fold_in(streams_of[6], 1), 0, P_ROWS - 1).astype(jnp.int32),
        "tile_rel": set_ends(jax.random.randint(streams_of[7], (N_REL, N_DOM * E_TILES), 0, RELS_DEV), jax.random.fold_in(streams_of[7], 1), 0, RELS_DEV - 1).astype(jnp.int32),
        "live_tiles": draw_live_tiles(jax.random.fold_in(streams_of[14], 71), 0),
        "neg_tiles": set_ends(jax.random.randint(streams_of[9], (N_REL, N_DOM * NEG_TILES), 0, P_TILES), jax.random.fold_in(streams_of[9], 1), 0, P_TILES - 1).astype(jnp.int32),
        "bound_rows": set_ends(jax.random.randint(streams_of[10], (N_DOM * 2 * BND,), 0, P_ROWS), jax.random.fold_in(streams_of[10], 1), 0, P_ROWS - 1).astype(jnp.int32),
        "band_src": set_ends(jax.random.randint(streams_of[11], (N_REL, N_DOM * BAND_ROWS), 0, P_ROWS), jax.random.fold_in(streams_of[11], 1), 0, P_ROWS - 1).astype(jnp.int32),
        "band_dst": set_ends(jax.random.randint(streams_of[12], (N_REL, N_DOM * BAND_ROWS), 0, 2 * BND), jax.random.fold_in(streams_of[12], 1), 0, (2 * BND) - 1).astype(jnp.int32),
        "band_rel": set_ends(jax.random.randint(streams_of[13], (N_REL, N_DOM * BAND_TILES), 0, RELS_DEV), jax.random.fold_in(streams_of[13], 1), 0, RELS_DEV - 1).astype(jnp.int32),
    }


def edge_terms(q, target, negs, valid):
    pos = lax.optimization_barrier(jnp.sum(q.astype(jnp.float32) * target.astype(jnp.float32), axis=1))
    neg = jnp.einsum('ed,nd->en', q, negs, preferred_element_type=jnp.float32)
    dpos = -jax.nn.sigmoid(-pos) * valid
    dneg = (jax.nn.sigmoid(neg) * (valid / negs.shape[0])[:, None]).astype(jnp.bfloat16)
    dq = dpos[:, None] * target.astype(jnp.float32) + jnp.einsum('en,nd->ed', dneg, negs, preferred_element_type=jnp.float32)
    dtarget = dpos[:, None] * q.astype(jnp.float32)
    dnegs = jnp.einsum('en,ed->nd', dneg, q, preferred_element_type=jnp.float32)
    return (dq, dtarget, dnegs)

def reference(emb, emb_state, rel_weight, rel_state, swap_mask, src_rows, dst_rows, tile_rel, live_tiles, neg_tiles, bound_rows, band_src, band_dst, band_rel):
    blocks = emb.reshape(N_DOM, P_ROWS, D)
    bounds = bound_rows.reshape(N_DOM, 2 * BND)
    mask = swap_mask[0].astype(jnp.int32)
    tile_of_edge = (jnp.arange(E_ROWS) // TILE).astype(jnp.int32)

    def one_device(index, carry):
        grads, rel_grads = carry
        index = jnp.asarray(index).astype(jnp.int32)
        dom_index = (index // N_REL).astype(jnp.int32)
        rel_index = (index % N_REL).astype(jnp.int32)
        own = blocks[dom_index]
        partner = jnp.bitwise_xor(dom_index, mask).astype(jnp.int32)
        far = blocks[partner].astype(jnp.bfloat16)
        lower = jnp.maximum(dom_index - 1, 0).astype(jnp.int32)
        upper = jnp.minimum(dom_index + 1, N_DOM - 1).astype(jnp.int32)
        has_lower = (dom_index > 0).astype(jnp.float32)
        has_upper = (dom_index < N_DOM - 1).astype(jnp.float32)
        lower_list = bounds[lower][BND:]
        upper_list = bounds[upper][:BND]
        near = jnp.concatenate([blocks[lower][lower_list] * has_lower, blocks[upper][upper_list] * has_upper], axis=0).astype(jnp.bfloat16)
        weights = lax.dynamic_slice_in_dim(rel_weight, rel_index * RELS_DEV, RELS_DEV, 0)
        src = lax.dynamic_slice(src_rows, (rel_index, dom_index * E_ROWS), (1, E_ROWS))[0]
        dst = lax.dynamic_slice(dst_rows, (rel_index, dom_index * E_ROWS), (1, E_ROWS))[0]
        rel_tiles = lax.dynamic_slice(tile_rel, (rel_index, dom_index * E_TILES), (1, E_TILES))[0]
        neg_ids = lax.dynamic_slice(neg_tiles, (rel_index, dom_index * NEG_TILES), (1, NEG_TILES))[0]
        bsrc = lax.dynamic_slice(band_src, (rel_index, dom_index * BAND_ROWS), (1, BAND_ROWS))[0]
        bdst = lax.dynamic_slice(band_dst, (rel_index, dom_index * BAND_ROWS), (1, BAND_ROWS))[0]
        brel_tiles = lax.dynamic_slice(band_rel, (rel_index, dom_index * BAND_TILES), (1, BAND_TILES))[0]
        live = live_tiles[rel_index, dom_index]
        valid = (tile_of_edge < live).astype(jnp.float32)
        rel_edge = jnp.repeat(rel_tiles, TILE)
        rel_band = jnp.repeat(brel_tiles, TILE)
        rel_all = jnp.concatenate([rel_edge, rel_band])
        src_all = jnp.concatenate([src, bsrc])
        w_all = weights[rel_all]
        rows_all = own[src_all]
        q = (rows_all * w_all).astype(jnp.bfloat16)
        negs = far.reshape(P_TILES, TILE, D)[neg_ids].reshape(NEG, D)
        target = jnp.concatenate([far[dst], near[bdst]], axis=0)
        valid_all = jnp.concatenate([valid, jnp.ones((BAND_ROWS,), jnp.float32)])
        dq, dtarget, dnegs = edge_terms(q, target, negs, valid_all)
        own_grad = jnp.zeros((P_ROWS, D), jnp.float32).at[src_all].add(dq * w_all)
        rel_term = jnp.zeros((RELS_DEV, D), jnp.float32).at[rel_all].add(dq * rows_all)
        far_grad = jnp.zeros((P_ROWS, D), jnp.float32).at[dst].add(dtarget[:E_ROWS])
        far_grad = far_grad.reshape(P_TILES, TILE, D).at[neg_ids].add(dnegs.reshape(NEG_TILES, TILE, D)).reshape(P_ROWS, D)
        near_grad = jnp.zeros((2 * BND, D), jnp.float32).at[bdst].add(dtarget[E_ROWS:])
        grads = grads.at[dom_index].add(own_grad)
        grads = grads.at[partner].add(far_grad)
        grads = grads.at[lower, lower_list].add(near_grad[:BND] * has_lower)
        grads = grads.at[upper, upper_list].add(near_grad[BND:] * has_upper)
        rel_grads = rel_grads.at[rel_index].add(rel_term)
        return (grads, rel_grads)
    start = (jnp.zeros((N_DOM, P_ROWS, D), jnp.float32), jnp.zeros((N_REL, RELS_DEV, D), jnp.float32))
    grads, rel_grads = lax.fori_loop(0, N_DOM * N_REL, one_device, start)
    full_grad = grads.reshape(ENT, D)
    state_new = emb_state + lax.optimization_barrier(jnp.mean(full_grad * full_grad, axis=1))
    emb_new = emb - 0.25 * full_grad / jnp.sqrt(state_new)[:, None]
    rel_grad = rel_grads.reshape(RELS, D)
    rel_new = rel_weight - 0.25 * rel_grad / jnp.sqrt(rel_state + lax.optimization_barrier(jnp.mean(rel_grad * rel_grad, axis=1)))[:, None]
    return (emb_new, state_new, rel_new)
```

```python
import functools

import jax
import jax.numpy as jnp
from jax import lax
from jax.experimental import pallas as pl
from jax.experimental.pallas import tpu as pltpu
from jax.sharding import PartitionSpec as P

step_rate = 0.25
tile = 128
MESH = pl.DeviceIdType.MESH
f32 = jnp.float32
bf16 = jnp.bfloat16


def dot(a, b, dims):
    return lax.dot_general(a, b, (dims, ((), ())), preferred_element_type=f32)


def nn(a, b):
    return dot(a, b, ((1,), (0,)))


def nt(a, b):
    return dot(a, b, ((1,), (1,)))


def tn(a, b):
    return dot(a, b, ((0,), (0,)))


def flipped(index, distance):
    bit = 1
    out = index
    while bit <= distance:
        if distance & bit:
            out = out + bit * (1 - 2 * ((index // bit) % 2))
        bit *= 2
    return out


def hot(ids, count):
    rows = lax.broadcasted_iota(jnp.int32, (count, ids.shape[1]), 0)
    return jnp.where(rows == ids, 1.0, 0.0).astype(bf16)


def kernel(
    n_dom,
    n_rel,
    route,
    mask_ref,
    tile_rel,
    live_ref,
    neg_ids,
    band_rel,
    emb,
    weights,
    src,
    dst,
    bound,
    bsrc,
    bdst,
    g_out,
    gw_out,
    own,
    far,
    far_step,
    rim,
    near,
    near_out,
    near_back,
    fg_out,
    fg_in,
    lo_out,
    lo_in,
    back,
    g_all,
    gw_out_buf,
    gw_in,
    s_route,
    r_route,
    s_far,
    r_far,
    s_near,
    r_near,
    s_nback,
    r_nback,
    s_fg,
    r_fg,
    s_lo,
    r_lo,
    s_back,
    r_back,
    s_g,
    r_g,
    s_gw,
    r_gw,
):
    rows, width = emb.shape
    share = rows // n_rel
    half = rows // 2
    rel_count = weights.shape[0]
    n_edge = src.shape[1]
    n_band = bsrc.shape[1]
    n_all = n_edge + n_band
    n_neg = neg_ids.shape[1]
    dom = lax.axis_index("dom")
    rel = lax.axis_index("rel")
    levels = [1 << b for b in range(n_dom.bit_length() - 1)]
    partners = sorted(set(levels) | {distance for distance, _ in route})
    has_low = dom > 0
    has_high = dom < n_dom - 1
    peers = [lax.rem(rel + k, n_rel) for k in range(1, n_rel)]
    mine = pl.ds(pl.multiple_of(rel * share, share), share)

    barrier = pltpu.get_barrier_semaphore()
    for peer in peers:
        pl.semaphore_signal(barrier, inc=1, device_id=(dom, peer), device_id_type=MESH)
    for distance in partners:
        pl.semaphore_signal(
            barrier, inc=1, device_id=(flipped(dom, distance), rel), device_id_type=MESH
        )

    @pl.when(has_low)
    def _():
        pl.semaphore_signal(barrier, inc=1, device_id=(dom - 1, rel), device_id_type=MESH)

    @pl.when(has_high)
    def _():
        pl.semaphore_signal(barrier, inc=1, device_id=(dom + 1, rel), device_id_type=MESH)

    table = emb[...]
    own_bf = table.astype(bf16)
    own[...] = own_bf
    bound_hot = hot(bound[...], rows)
    rim[...] = tn(bound_hot, own_bf).astype(bf16)

    sides = (dom + n_dom - 1) // n_dom + 1 - dom // (n_dom - 1)
    pl.semaphore_wait(barrier, len(peers) + len(partners) + sides)

    def remote(source, target, send, recv, device):
        return pltpu.make_async_remote_copy(
            src_ref=source,
            dst_ref=target,
            send_sem=send,
            recv_sem=recv,
            device_id=device,
            device_id_type=MESH,
        )

    def route_copy(buffer, first, step, sends, recvs):
        distance, _ = route[step]
        source = first if step == 0 else buffer.at[2 * step]
        return remote(
            source,
            buffer.at[2 * step + 1],
            sends.at[step],
            recvs.at[step],
            (flipped(dom, distance), rel),
        )

    def routed(buffer, first, step):
        got = buffer[2 * step + 1].astype(f32)
        bit = route[step][1]
        if bit is None:
            return got
        held = (first[...] if step == 0 else buffer[2 * step]).astype(f32)
        moved = (mask_ref[0] // (1 << bit)) % 2
        return jnp.where(moved == 1, got, held)

    first_share = own.at[mine]
    out_copy = route_copy(far_step, first_share, 0, s_route, r_route)
    out_copy.start()

    def low_copy(source, target, sends, recvs):
        return remote(
            source.at[pl.ds(0, half)],
            target.at[pl.ds(half, half)],
            sends.at[0],
            recvs.at[1],
            (dom - 1, rel),
        )

    def high_copy(source, target, sends, recvs):
        return remote(
            source.at[pl.ds(half, half)],
            target.at[pl.ds(0, half)],
            sends.at[1],
            recvs.at[0],
            (dom + 1, rel),
        )

    def near_start(source, target, sends, recvs):
        @pl.when(has_low)
        def _():
            low_copy(source, target, sends, recvs).start()

        @pl.when(has_high)
        def _():
            high_copy(source, target, sends, recvs).start()

    def near_wait(source, target, sends, recvs):
        @pl.when(has_low)
        def _():
            low_copy(source, target, sends, recvs).wait_send()
            high_copy(source, target, sends, recvs).wait_recv()

        @pl.when(has_high)
        def _():
            high_copy(source, target, sends, recvs).wait_send()
            low_copy(source, target, sends, recvs).wait_recv()

        @pl.when(dom == 0)
        def _():
            target[pl.ds(0, half), :] = jnp.zeros((half, width), bf16)

        @pl.when(dom == n_dom - 1)
        def _():
            target[pl.ds(half, half), :] = jnp.zeros((half, width), bf16)

    near_start(rim, near, s_near, r_near)

    src_all = jnp.concatenate([src[...], bsrc[...]], axis=1)
    src_hot = hot(src_all, rows)
    low_part = (table - own_bf.astype(f32)).astype(bf16)
    rows_t = tn(own_bf, src_hot) + tn(low_part, src_hot)
    ids = jnp.concatenate(
        [jnp.full((1, tile), tile_rel[0, t], jnp.int32) for t in range(n_edge // tile)]
        + [jnp.full((1, tile), band_rel[0, t], jnp.int32) for t in range(n_band // tile)],
        axis=1,
    )
    stack = 4 * rel_count
    id_rows = lax.broadcasted_iota(jnp.int32, (stack, n_all), 0) % rel_count
    rel_hot = jnp.where(id_rows == ids, 1.0, 0.0).astype(bf16)
    w = weights[...]
    w_1 = w.astype(bf16).astype(f32)
    w_2 = (w - w_1).astype(bf16).astype(f32)
    w_3 = w - w_1 - w_2
    w_stack = jnp.concatenate([w_1, w_2, w_3, jnp.zeros_like(w)], axis=0).astype(bf16)
    w_t = tn(w_stack, rel_hot)
    q = (rows_t * w_t).astype(bf16)
    q_f = q.astype(f32)

    def edge_pos(edges, target_t, valid):
        pos = jnp.sum(q_f[:, edges] * target_t, axis=0, keepdims=True)
        dpos = -valid / (1.0 + jnp.exp(pos))
        return dpos, (dpos * q_f[:, edges]).astype(bf16)

    def band_part():
        near_wait(rim, near, s_near, r_near)
        bdst_hot = hot(bdst[...], rows)
        target_t = tn(near[...], bdst_hot)
        dpos, dtarget = edge_pos(slice(n_edge, n_all), target_t, jnp.ones((1, n_band), f32))
        near_out[...] = nt(bdst_hot, dtarget).astype(bf16)
        near_start(near_out, near_back, s_nback, r_nback)
        return dpos * target_t

    band_dq = None
    for step in range(len(route)):
        out_copy.wait()
        moved = routed(far_step, first_share, step).astype(bf16)
        if step < len(route) - 1:
            far_step[2 * step + 2] = moved
            out_copy = route_copy(far_step, first_share, step + 1, s_route, r_route)
            out_copy.start()
            if step == 0:
                band_dq = band_part()
        else:
            far[mine, :] = moved

    def spread(buffer, sends, recvs):
        return [
            remote(
                buffer.at[mine], buffer.at[mine], sends.at[k], recvs.at[k], (dom, peer)
            )
            for k, peer in enumerate(peers)
        ]

    far_copies = spread(far, s_far, r_far)
    for copy in far_copies:
        copy.start()
    if band_dq is None:
        band_dq = band_part()
    dst_hot = hot(dst[...], rows)
    edge_ids = lax.broadcasted_iota(jnp.int32, (1, n_all), 1)
    limit = live_ref[0, 0] * tile
    valid = jnp.where((edge_ids < limit) | (edge_ids >= n_edge), 1.0, 0.0)
    row_tile = lax.broadcasted_iota(jnp.int32, (rows, 1), 0) // tile
    counts = jnp.zeros((rows, 1), f32)
    for k in range(n_neg):
        counts = counts + jnp.where(row_tile == neg_ids[0, k], 1.0, 0.0)
    scale = counts * (1.0 / (n_neg * tile))
    for copy in far_copies:
        copy.wait()

    far_rows = far[...]
    neg = nn(far_rows, q)
    dneg = (valid * scale / (1.0 + jnp.exp(-neg))).astype(bf16)
    target_t = tn(far_rows, dst_hot)
    dpos, dtarget = edge_pos(slice(0, n_edge), target_t, valid[:, :n_edge])
    far_grad = nt(dst_hot, dtarget) + nt(dneg, q)
    fg_out[...] = far_grad.astype(bf16)

    def scatter(source, target, sends, recvs):
        return [
            remote(
                source.at[pl.ds(pl.multiple_of(peer * share, share), share)],
                target.at[k],
                sends.at[k],
                recvs.at[k],
                (dom, peer),
            )
            for k, peer in enumerate(peers)
        ]

    fg_copies = scatter(fg_out, fg_in, s_fg, r_fg)
    for copy in fg_copies:
        copy.start()

    dq = jnp.concatenate([dpos * target_t, band_dq], axis=1) + tn(far_rows, dneg)
    own_grad = nt(src_hot, (dq * w_t).astype(bf16))
    near_wait(near_out, near_back, s_nback, r_nback)
    lo_out[...] = (own_grad + nn(bound_hot, near_back[...])).astype(bf16)
    lo_copies = scatter(lo_out, lo_in, s_lo, r_lo)
    for copy in lo_copies:
        copy.start()

    gw = nt(rel_hot, (dq * rows_t).astype(bf16))[:rel_count]

    def gw_copy(level):
        return remote(
            gw_out_buf.at[level],
            gw_in.at[level],
            s_gw.at[level],
            r_gw.at[level],
            (flipped(dom, levels[level]), rel),
        )

    gw_out_buf[0] = gw
    gw_copy(0).start()

    for copy in fg_copies:
        copy.wait()
    total = fg_out[mine, :].astype(f32)
    for k in range(n_rel - 1):
        total = total + fg_in[k].astype(f32)
    back[0] = total.astype(bf16)
    back_copy = route_copy(back, back.at[0], 0, s_back, r_back)
    back_copy.start()

    for copy in lo_copies:
        copy.wait()
    local = lo_out[mine, :].astype(f32)
    for k in range(n_rel - 1):
        local = local + lo_in[k].astype(f32)

    for step in range(len(route)):
        back_copy.wait()
        total = routed(back, back.at[0], step)
        if step < len(route) - 1:
            back[2 * step + 2] = total.astype(bf16)
            back_copy = route_copy(back, back.at[0], step + 1, s_back, r_back)
            back_copy.start()
    g_all[mine, :] = (local + total).astype(bf16)
    g_copies = spread(g_all, s_g, r_g)
    for copy in g_copies:
        copy.start()

    for level in range(len(levels)):
        gw_copy(level).wait()
        gw = gw_out_buf[level] + gw_in[level]
        if level < len(levels) - 1:
            gw_out_buf[level + 1] = gw
            gw_copy(level + 1).start()
    gw_out[...] = gw

    for copy in g_copies:
        copy.wait()
    g_out[...] = g_all[...].astype(f32)


def gradients(n_dom, n_rel, route, collective_id, args):
    emb, weights = args[5], args[6]
    rows, width = emb.shape
    rel_count = weights.shape[0]
    share = rows // n_rel
    peers = n_rel - 1
    levels = n_dom.bit_length() - 1
    steps = len(route)
    table = pltpu.VMEM((rows, width), bf16)
    pair = pltpu.SemaphoreType.DMA((2,))
    to_peers = pltpu.SemaphoreType.DMA((peers,))
    per_step = pltpu.SemaphoreType.DMA((steps,))
    per_level = pltpu.SemaphoreType.DMA((levels,))
    part = pltpu.VMEM((peers, share, width), bf16)
    hops = pltpu.VMEM((2 * steps, share, width), bf16)
    smem = pl.BlockSpec(memory_space=pltpu.SMEM)
    vmem = pl.BlockSpec(memory_space=pltpu.VMEM)
    return pl.pallas_call(
        functools.partial(kernel, n_dom, n_rel, route),
        out_shape=(
            jax.ShapeDtypeStruct((rows, width), f32),
            jax.ShapeDtypeStruct((rel_count, width), f32),
        ),
        in_specs=[smem] * 5 + [vmem] * 7,
        out_specs=(vmem, vmem),
        scratch_shapes=[
            table,
            table,
            hops,
            table,
            table,
            table,
            table,
            table,
            part,
            table,
            part,
            hops,
            table,
            pltpu.VMEM((levels, rel_count, width), f32),
            pltpu.VMEM((levels, rel_count, width), f32),
            per_step,
            per_step,
            to_peers,
            to_peers,
            pair,
            pair,
            pair,
            pair,
            to_peers,
            to_peers,
            to_peers,
            to_peers,
            per_step,
            per_step,
            to_peers,
            to_peers,
            per_level,
            per_level,
        ],
        compiler_params=pltpu.CompilerParams(
            collective_id=collective_id,
            has_side_effects=True,
            vmem_limit_bytes=48 * 1024 * 1024,
        ),
    )(*args)


def adagrad(table, state, grad):
    fresh = state + jnp.mean(grad * grad, axis=1)
    return (table - step_rate * grad / jnp.sqrt(fresh)[:, None], fresh)


def body(
    emb,
    emb_state,
    rel_weight,
    rel_state,
    swap_mask,
    src_rows,
    dst_rows,
    tile_rel,
    live_tiles,
    neg_tiles,
    bound_rows,
    band_src,
    band_dst,
    band_rel,
):
    n_dom = lax.axis_size("dom")
    n_rel = lax.axis_size("rel")
    args = (
        swap_mask,
        tile_rel,
        live_tiles,
        neg_tiles,
        band_rel,
        emb,
        rel_weight,
        src_rows,
        dst_rows,
        bound_rows.reshape(1, -1),
        band_src,
        band_dst,
    )
    route = [(1 << bit, bit) for bit in range(n_dom.bit_length() - 1)]
    grad, rel_grad = gradients(n_dom, n_rel, route, 0, args)
    emb_new, state_new = adagrad(emb, emb_state, grad)
    rel_new, _ = adagrad(rel_weight, rel_state, rel_grad)
    return (emb_new, state_new, rel_new)


def solution(mesh):
    in_specs = (
        P("dom", None),
        P("dom"),
        P("rel", None),
        P("rel"),
        P(),
        P("rel", "dom"),
        P("rel", "dom"),
        P("rel", "dom"),
        P("rel", "dom"),
        P("rel", "dom"),
        P("dom"),
        P("rel", "dom"),
        P("rel", "dom"),
        P("rel", "dom"),
    )
    out_specs = (P("dom", None), P("dom"), P("rel", None))
    return jax.shard_map(body, mesh=mesh, in_specs=in_specs, out_specs=out_specs, check_vma=False)
```

```python
import functools

import jax
import jax.numpy as jnp
from jax import lax
from jax.experimental import pallas as pl
from jax.experimental.pallas import tpu as pltpu
from jax.sharding import PartitionSpec as P

step_rate = 0.25
tile = 128
MESH = pl.DeviceIdType.MESH
f32 = jnp.float32
bf16 = jnp.bfloat16


def dot(a, b, dims):
    return lax.dot_general(a, b, (dims, ((), ())), preferred_element_type=f32)


def nn(a, b):
    return dot(a, b, ((1,), (0,)))


def nt(a, b):
    return dot(a, b, ((1,), (1,)))


def tn(a, b):
    return dot(a, b, ((0,), (0,)))


def flipped(index, distance):
    bit = 1
    out = index
    while bit <= distance:
        if distance & bit:
            out = out + bit * (1 - 2 * ((index // bit) % 2))
        bit *= 2
    return out


def hot(ids, count):
    rows = lax.broadcasted_iota(jnp.int32, (count, ids.shape[1]), 0)
    return jnp.where(rows == ids, 1.0, 0.0).astype(bf16)


def kernel(
    n_dom,
    n_rel,
    route,
    mask_ref,
    tile_rel,
    live_ref,
    neg_ids,
    band_rel,
    emb_t,
    state,
    weights,
    rel_state,
    src,
    dst,
    bound,
    bsrc,
    bdst,
    emb_out,
    state_out,
    rel_out,
    own,
    far,
    far_step,
    rim,
    near,
    near_out,
    pair_in,
    near_sum,
    near_back,
    fg_keep,
    fg_out,
    fg_in,
    lo_keep,
    lo_out,
    lo_in,
    back,
    g_all,
    gw_out_buf,
    gw_in,
    s_route,
    r_route,
    s_far,
    r_far,
    s_near,
    r_near,
    s_mate,
    r_mate,
    s_pair,
    r_pair,
    s_nback,
    r_nback,
    s_fg,
    r_fg,
    s_lo,
    r_lo,
    s_back,
    r_back,
    s_g,
    r_g,
    s_gw,
    r_gw,
):
    width, rows = emb_t.shape
    share = rows // n_rel
    half = rows // 2
    chunk = half // 2
    rel_count = weights.shape[0]
    n_edge = src.shape[1]
    n_band = bsrc.shape[1]
    n_all = n_edge + n_band
    n_neg = neg_ids.shape[1]
    dom = lax.axis_index("dom")
    rel = lax.axis_index("rel")
    levels = [1 << b for b in range(n_dom.bit_length() - 1)]
    partners = sorted(set(levels) | {distance for distance, _ in route})
    has_low = dom > 0
    has_high = dom < n_dom - 1
    peers = [lax.rem(rel + k, n_rel) for k in range(1, n_rel)]
    mine = pl.ds(pl.multiple_of(rel * share, share), share)
    core = lax.rem(rel, 2)
    mate = rel + 1 - 2 * core
    core_rows = pl.ds(pl.multiple_of(core * half, half), half)

    def chunk_of(side, which):
        return pl.ds(pl.multiple_of(side * half + which * chunk, chunk), chunk)

    near[...] = jnp.zeros_like(near)
    near_back[...] = jnp.zeros_like(near_back)

    barrier = pltpu.get_barrier_semaphore()
    for peer in peers:
        pl.semaphore_signal(barrier, inc=1, device_id=(dom, peer), device_id_type=MESH)
    for distance in partners:
        pl.semaphore_signal(
            barrier, inc=1, device_id=(flipped(dom, distance), rel), device_id_type=MESH
        )

    @pl.when(has_low)
    def _():
        pl.semaphore_signal(barrier, inc=1, device_id=(dom - 1, rel), device_id_type=MESH)

    @pl.when(has_high)
    def _():
        pl.semaphore_signal(barrier, inc=1, device_id=(dom + 1, rel), device_id_type=MESH)

    table = emb_t[...]
    own_t = table.astype(bf16)
    eye = hot(lax.broadcasted_iota(jnp.int32, (1, rows), 1), rows)
    own[...] = nt(eye, own_t).astype(bf16)
    bound_hot = hot(bound[...], rows)
    rim[...] = tn(bound_hot, own[...]).astype(bf16)

    sides = (dom + n_dom - 1) // n_dom + 1 - dom // (n_dom - 1)
    pl.semaphore_wait(barrier, len(peers) + len(partners) + sides)

    def remote(source, target, send, recv, device):
        return pltpu.make_async_remote_copy(
            src_ref=source,
            dst_ref=target,
            send_sem=send,
            recv_sem=recv,
            device_id=device,
            device_id_type=MESH,
        )

    def route_copy(buffer, first, step, sends, recvs):
        distance, _ = route[step]
        source = first if step == 0 else buffer.at[2 * step]
        return remote(
            source,
            buffer.at[2 * step + 1],
            sends.at[step],
            recvs.at[step],
            (flipped(dom, distance), rel),
        )

    def routed(buffer, first, step):
        got = buffer[2 * step + 1].astype(f32)
        bit = route[step][1]
        if bit is None:
            return got
        held = (first[...] if step == 0 else buffer[2 * step]).astype(f32)
        moved = (mask_ref[0] // (1 << bit)) % 2
        return jnp.where(moved == 1, got, held)

    first_share = own.at[core_rows]
    out_copy = route_copy(far_step, first_share, 0, s_route, r_route)
    out_copy.start()

    def low_copy(source, target, sends, recvs):
        return remote(source, target, sends.at[0], recvs.at[1], (dom - 1, rel))

    def high_copy(source, target, sends, recvs):
        return remote(source, target, sends.at[1], recvs.at[0], (dom + 1, rel))

    def sides_of(source, target):
        low = (source.at[chunk_of(0, core)], target.at[chunk_of(1, core)])
        high = (source.at[chunk_of(1, core)], target.at[chunk_of(0, core)])
        return low, high

    def near_start(source, target, sends, recvs):
        low, high = sides_of(source, target)

        @pl.when(has_low)
        def _():
            low_copy(*low, sends, recvs).start()

        @pl.when(has_high)
        def _():
            high_copy(*high, sends, recvs).start()

    def near_wait(source, target, sends, recvs):
        low, high = sides_of(source, target)

        @pl.when(has_low)
        def _():
            low_copy(*low, sends, recvs).wait_send()
            high_copy(*high, sends, recvs).wait_recv()

        @pl.when(has_high)
        def _():
            high_copy(*high, sends, recvs).wait_send()
            low_copy(*low, sends, recvs).wait_recv()

    def mate_copy(side):
        block = near.at[chunk_of(side, core)]
        return remote(block, block, s_mate.at[side], r_mate.at[side], (dom, mate))

    def pair_copy(side):
        return remote(
            near_out.at[chunk_of(side, 1 - core)],
            pair_in.at[side],
            s_pair.at[side],
            r_pair.at[side],
            (dom, mate),
        )

    near_start(rim, near, s_near, r_near)

    src_all = jnp.concatenate([src[...], bsrc[...]], axis=1)
    src_hot = hot(src_all, rows)
    low_part = (table - own_t.astype(f32)).astype(bf16)
    rows_t = nn(own_t, src_hot) + nn(low_part, src_hot)
    ids = jnp.concatenate(
        [jnp.full((1, tile), tile_rel[0, t], jnp.int32) for t in range(n_edge // tile)]
        + [jnp.full((1, tile), band_rel[0, t], jnp.int32) for t in range(n_band // tile)],
        axis=1,
    )
    stack = 4 * rel_count
    id_rows = lax.broadcasted_iota(jnp.int32, (stack, n_all), 0) % rel_count
    rel_hot = jnp.where(id_rows == ids, 1.0, 0.0).astype(bf16)
    w = weights[...]
    w_1 = w.astype(bf16).astype(f32)
    w_2 = (w - w_1).astype(bf16).astype(f32)
    w_3 = w - w_1 - w_2
    w_stack = jnp.concatenate([w_1, w_2, w_3, jnp.zeros_like(w)], axis=0).astype(bf16)
    w_t = tn(w_stack, rel_hot)
    q = (rows_t * w_t).astype(bf16)
    q_f = q.astype(f32)

    def edge_pos(edges, target_t, valid):
        pos = jnp.sum(q_f[:, edges] * target_t, axis=0, keepdims=True)
        dpos = -valid / (1.0 + jnp.exp(pos))
        return dpos, (dpos * q_f[:, edges]).astype(bf16)

    near_wait(rim, near, s_near, r_near)

    def mates(act):
        @pl.when(has_low)
        def _():
            act(mate_copy(0))

        @pl.when(has_high)
        def _():
            act(mate_copy(1))

    mates(lambda copy: copy.start())

    for step in range(len(route)):
        out_copy.wait()
        moved = routed(far_step, first_share, step).astype(bf16)
        if step < len(route) - 1:
            far_step[2 * step + 2] = moved
            out_copy = route_copy(far_step, first_share, step + 1, s_route, r_route)
            out_copy.start()
        else:
            far[core_rows, :] = moved
    far_copy = remote(
        far.at[core_rows], far.at[core_rows], s_far.at[0], r_far.at[0], (dom, mate)
    )
    far_copy.start()

    def spread(buffer, sends, recvs):
        return [
            remote(
                buffer.at[mine], buffer.at[mine], sends.at[k], recvs.at[k], (dom, peer)
            )
            for k, peer in enumerate(peers)
        ]

    mates(lambda copy: copy.wait())
    bdst_hot = hot(bdst[...], rows)
    near_t = tn(near[...], bdst_hot)
    band_dpos, band_dtarget = edge_pos(slice(n_edge, n_all), near_t, jnp.ones((1, n_band), f32))
    near_out[...] = nt(bdst_hot, band_dtarget).astype(bf16)
    pair_copies = [pair_copy(0), pair_copy(1)]
    for copy in pair_copies:
        copy.start()
    band_dq = band_dpos * near_t

    dst_hot = hot(dst[...], rows)
    edge_ids = lax.broadcasted_iota(jnp.int32, (1, n_all), 1)
    limit = live_ref[0, 0] * tile
    valid = jnp.where((edge_ids < limit) | (edge_ids >= n_edge), 1.0, 0.0)
    row_tile = lax.broadcasted_iota(jnp.int32, (rows, 1), 0) // tile
    counts = jnp.zeros((rows, 1), f32)
    for k in range(n_neg):
        counts = counts + jnp.where(row_tile == neg_ids[0, k], 1.0, 0.0)
    scale = counts * (1.0 / (n_neg * tile))
    for side, copy in enumerate(pair_copies):
        copy.wait()
        block = chunk_of(side, core)
        total = near_out[block, :].astype(f32) + pair_in[side].astype(f32)
        near_sum[block, :] = total.astype(bf16)
    near_start(near_sum, near_back, s_nback, r_nback)
    far_copy.wait()

    far_rows = far[...]
    neg = nn(far_rows, q)
    dneg = (valid * scale / (1.0 + jnp.exp(-neg))).astype(bf16)
    target_t = tn(far_rows, dst_hot)
    dpos, dtarget = edge_pos(slice(0, n_edge), target_t, valid[:, :n_edge])
    far_grad = nt(dst_hot, dtarget) + nt(dneg, q)
    fg_keep[...] = far_grad
    fg_out[...] = far_grad.astype(bf16)

    def scatter(source, target, sends, recvs):
        return [
            remote(
                source.at[pl.ds(pl.multiple_of(peer * share, share), share)],
                target.at[k],
                sends.at[k],
                recvs.at[k],
                (dom, peer),
            )
            for k, peer in enumerate(peers)
        ]

    fg_copies = scatter(fg_out, fg_in, s_fg, r_fg)
    for copy in fg_copies:
        copy.start()

    dq = jnp.concatenate([dpos * target_t, band_dq], axis=1) + tn(far_rows, dneg)
    own_grad = nt(src_hot, (dq * w_t).astype(bf16))
    near_wait(near_sum, near_back, s_nback, r_nback)
    local_grad = own_grad + nn(bound_hot, near_back[...])
    lo_keep[...] = local_grad
    lo_out[...] = local_grad.astype(bf16)
    lo_copies = scatter(lo_out, lo_in, s_lo, r_lo)
    for copy in lo_copies:
        copy.start()

    gw = nt(rel_hot, (dq * rows_t).astype(bf16))[:rel_count]

    def gw_copy(level):
        return remote(
            gw_out_buf.at[level],
            gw_in.at[level],
            s_gw.at[level],
            r_gw.at[level],
            (flipped(dom, levels[level]), rel),
        )

    gw_out_buf[0] = gw
    gw_copy(0).start()

    for copy in fg_copies:
        copy.wait()
    total = fg_keep[mine, :]
    for k in range(n_rel - 1):
        total = total + fg_in[k].astype(f32)
    back[0] = total.astype(bf16)
    back_copy = route_copy(back, back.at[0], 0, s_back, r_back)
    back_copy.start()

    for copy in lo_copies:
        copy.wait()
    local = lo_keep[mine, :]
    for k in range(n_rel - 1):
        local = local + lo_in[k].astype(f32)

    for step in range(len(route)):
        back_copy.wait()
        total = routed(back, back.at[0], step)
        if step < len(route) - 1:
            back[2 * step + 2] = total.astype(bf16)
            back_copy = route_copy(back, back.at[0], step + 1, s_back, r_back)
            back_copy.start()
    g_all[mine, :] = (local + total).astype(bf16)
    g_copies = spread(g_all, s_g, r_g)
    for copy in g_copies:
        copy.start()

    for level in range(len(levels)):
        gw_copy(level).wait()
        gw = gw_out_buf[level] + gw_in[level]
        if level < len(levels) - 1:
            gw_out_buf[level + 1] = gw
            gw_copy(level + 1).start()
    eye_rel = lax.broadcasted_iota(jnp.int32, (rel_count, rel_count), 0) == (
        lax.broadcasted_iota(jnp.int32, (rel_count, rel_count), 1)
    )
    rel_col = jnp.sum(jnp.where(eye_rel, rel_state[...], 0.0), axis=1, keepdims=True)
    rel_fresh = rel_col + jnp.mean(gw * gw, axis=1, keepdims=True)
    rel_out[...] = weights[...] - step_rate * gw / jnp.sqrt(rel_fresh)

    for copy in g_copies:
        copy.wait()
    grad_t = tn(g_all[...], eye)
    fresh = state[...] + jnp.sum(grad_t * grad_t, axis=0, keepdims=True) * (1.0 / width)
    state_out[...] = fresh
    emb_out[...] = emb_t[...] - grad_t * (step_rate / jnp.sqrt(fresh))


def updates(n_dom, n_rel, route, collective_id, args):
    emb_t, weights = args[5], args[7]
    width, rows = emb_t.shape
    rel_count = weights.shape[0]
    share = rows // n_rel
    peers = n_rel - 1
    levels = n_dom.bit_length() - 1
    steps = len(route)
    table = pltpu.VMEM((rows, width), bf16)
    wide = pltpu.VMEM((rows, width), f32)
    one = pltpu.SemaphoreType.DMA((1,))
    pair = pltpu.SemaphoreType.DMA((2,))
    to_peers = pltpu.SemaphoreType.DMA((peers,))
    per_step = pltpu.SemaphoreType.DMA((steps,))
    per_level = pltpu.SemaphoreType.DMA((levels,))
    part = pltpu.VMEM((peers, share, width), bf16)
    small = pltpu.VMEM((levels, rel_count, width), f32)
    smem = pl.BlockSpec(memory_space=pltpu.SMEM)
    vmem = pl.BlockSpec(memory_space=pltpu.VMEM)
    semaphores = [per_step, one, pair, pair, pair, pair, to_peers, to_peers, per_step, to_peers]
    semaphores = [kind for kind in semaphores + [per_level] for _ in range(2)]
    return pl.pallas_call(
        functools.partial(kernel, n_dom, n_rel, route),
        out_shape=(
            jax.ShapeDtypeStruct((width, rows), f32),
            jax.ShapeDtypeStruct((1, rows), f32),
            jax.ShapeDtypeStruct((rel_count, width), f32),
        ),
        in_specs=[smem] * 5 + [vmem] * 9,
        out_specs=(vmem, vmem, vmem),
        scratch_shapes=[
            table,
            table,
            pltpu.VMEM((2 * steps, rows // 2, width), bf16),
            table,
            table,
            table,
            pltpu.VMEM((2, rows // 4, width), bf16),
            table,
            table,
            wide,
            table,
            part,
            wide,
            table,
            part,
            pltpu.VMEM((2 * steps, share, width), bf16),
            table,
            small,
            small,
        ]
        + semaphores,
        compiler_params=pltpu.CompilerParams(
            collective_id=collective_id,
            has_side_effects=True,
            vmem_limit_bytes=48 * 1024 * 1024,
        ),
    )(*args)


def body(
    emb,
    emb_state,
    rel_weight,
    rel_state,
    swap_mask,
    src_rows,
    dst_rows,
    tile_rel,
    live_tiles,
    neg_tiles,
    bound_rows,
    band_src,
    band_dst,
    band_rel,
):
    n_dom = lax.axis_size("dom")
    n_rel = lax.axis_size("rel")
    args = (
        swap_mask,
        tile_rel,
        live_tiles,
        neg_tiles,
        band_rel,
        emb.T,
        emb_state.reshape(1, -1),
        rel_weight,
        rel_state.reshape(1, -1),
        src_rows,
        dst_rows,
        bound_rows.reshape(1, -1),
        band_src,
        band_dst,
    )
    if n_dom <= 8:
        branches = [
            functools.partial(updates, n_dom, n_rel, [(m, None)], m) for m in range(1, n_dom)
        ]
        emb_t, state_new, rel_new = lax.switch(swap_mask[0] - 1, branches, args)
    else:
        route = [(1 << bit, bit) for bit in range(n_dom.bit_length() - 1)]
        emb_t, state_new, rel_new = updates(n_dom, n_rel, route, 0, args)
    return (emb_t.T, state_new.reshape(-1), rel_new)


def solution(mesh):
    in_specs = (
        P("dom", None),
        P("dom"),
        P("rel", None),
        P("rel"),
        P(),
        P("rel", "dom"),
        P("rel", "dom"),
        P("rel", "dom"),
        P("rel", "dom"),
        P("rel", "dom"),
        P("dom"),
        P("rel", "dom"),
        P("rel", "dom"),
        P("rel", "dom"),
    )
    out_specs = (P("dom", None), P("dom"), P("rel", None))
    return jax.shard_map(body, mesh=mesh, in_specs=in_specs, out_specs=out_specs, check_vma=False)
```

```python
import functools

import jax
import jax.numpy as jnp
from jax import lax
from jax.experimental import pallas as pl
from jax.experimental.pallas import tpu as pltpu
from jax.sharding import PartitionSpec as P

step_rate = 0.25
tile = 128
MESH = pl.DeviceIdType.MESH
f32 = jnp.float32
bf16 = jnp.bfloat16


def dot(a, b, dims):
    return lax.dot_general(a, b, (dims, ((), ())), preferred_element_type=f32)


def nn(a, b):
    return dot(a, b, ((1,), (0,)))


def nt(a, b):
    return dot(a, b, ((1,), (1,)))


def tn(a, b):
    return dot(a, b, ((0,), (0,)))


def flipped(index, distance):
    bit = 1
    out = index
    while bit <= distance:
        if distance & bit:
            out = out + bit * (1 - 2 * ((index // bit) % 2))
        bit *= 2
    return out


def hot(ids, count):
    rows = lax.broadcasted_iota(jnp.int32, (count, ids.shape[1]), 0)
    return jnp.where(rows == ids, 1.0, 0.0).astype(bf16)


def kernel(
    n_dom,
    n_rel,
    route,
    mask_ref,
    tile_rel,
    live_ref,
    neg_ids,
    band_rel,
    emb_t,
    state,
    weights,
    rel_state,
    src,
    dst,
    bound,
    bsrc,
    bdst,
    emb_out,
    state_out,
    rel_out,
    own,
    far,
    far_step,
    rim,
    near,
    near_out,
    pair_in,
    near_sum,
    near_back,
    fg_keep,
    fg_out,
    fg_in,
    lo_keep,
    lo_out,
    lo_in,
    back,
    g_all,
    q_all,
    dt_all,
    gw_out,
    gw_in,
    s_route,
    r_route,
    s_far,
    r_far,
    s_near,
    r_near,
    s_mate,
    r_mate,
    s_pair,
    r_pair,
    s_nback,
    r_nback,
    s_fg,
    r_fg,
    s_lo,
    r_lo,
    s_back,
    r_back,
    s_g,
    r_g,
    s_gw,
    r_gw,
):
    width, rows = emb_t.shape
    half = rows // 2
    n_y = n_rel // 2
    padded = g_all.shape[0]
    part = padded // n_y
    rel_count = weights.shape[0]
    n_edge = src.shape[1]
    n_band = bsrc.shape[1]
    n_all = n_edge + n_band
    n_neg = neg_ids.shape[1]
    dom = lax.axis_index("dom")
    rel = lax.axis_index("rel")
    y = rel // 2
    core = rel % 2
    mate = rel + 1 - 2 * core
    levels = [1 << b for b in range(n_dom.bit_length() - 1)]
    partners = sorted(set(levels) | {distance for distance, _ in route})
    direct = route[0][1] is None
    has_low = (dom + n_dom - 1) // n_dom
    has_high = 1 - dom // (n_dom - 1)
    sends_near = core * has_high + (1 - core) * has_low
    hears_near = core * has_low + (1 - core) * has_high
    beside = dom + 2 * core - 1
    peers = [lax.rem(rel + k, n_rel) for k in range(1, n_rel)]

    def lanes(which):
        return pl.ds(pl.multiple_of(which * half, half), half)

    def down(which):
        return pl.ds(pl.multiple_of(which * part, part), part)

    near_back[...] = jnp.zeros_like(near_back)
    near[...] = jnp.zeros_like(near)

    barrier = pltpu.get_barrier_semaphore()
    for peer in peers:
        pl.semaphore_signal(barrier, inc=1, device_id=(dom, peer), device_id_type=MESH)
    for distance in partners:
        pl.semaphore_signal(
            barrier, inc=1, device_id=(flipped(dom, distance), rel), device_id_type=MESH
        )

    @pl.when(has_low == 1)
    def _():
        pl.semaphore_signal(barrier, inc=1, device_id=(dom - 1, rel), device_id_type=MESH)

    @pl.when(has_high == 1)
    def _():
        pl.semaphore_signal(barrier, inc=1, device_id=(dom + 1, rel), device_id_type=MESH)

    table = emb_t[...]
    own_t = table.astype(bf16)
    own[...] = own_t
    pl.semaphore_wait(barrier, len(peers) + len(partners) + has_low + has_high)

    def remote(source, target, send, recv, device):
        return pltpu.make_async_remote_copy(
            src_ref=source,
            dst_ref=target,
            send_sem=send,
            recv_sem=recv,
            device_id=device,
            device_id_type=MESH,
        )

    def route_copy(buffer, first, step, sends, recvs, last):
        distance, _ = route[step]
        return remote(
            first if step == 0 else buffer.at[2 * step],
            last if direct else buffer.at[2 * step + 1],
            sends.at[step],
            recvs.at[step],
            (flipped(dom, distance), rel),
        )

    def routed(buffer, first, step):
        got = buffer[2 * step + 1].astype(f32)
        held = (first[...] if step == 0 else buffer[2 * step]).astype(f32)
        moved = (mask_ref[0] // (1 << route[step][1])) % 2
        return jnp.where(moved == 1, got, held)

    own_half = own.at[:, lanes(core)]
    far_half = far.at[:, lanes(core)]
    out_copy = route_copy(far_step, own_half, 0, s_route, r_route, far_half)
    out_copy.start()

    bound_hot = hot(bound[...], rows)
    rim[...] = nn(own_t, bound_hot).astype(bf16)
    near_copy = remote(
        rim.at[:, lanes(core)], near.at[:, lanes(1 - core)], s_near.at[0], r_near.at[0], (beside, rel)
    )

    @pl.when(sends_near == 1)
    def _():
        near_copy.start()

    src_all = jnp.concatenate([src[...], bsrc[...]], axis=1)
    src_hot = hot(src_all, rows)
    low_part = (table - own_t.astype(f32)).astype(bf16)
    rows_t = nn(own_t, src_hot) + nn(low_part, src_hot)
    ids = jnp.concatenate(
        [jnp.full((1, tile), tile_rel[0, t], jnp.int32) for t in range(n_edge // tile)]
        + [jnp.full((1, tile), band_rel[0, t], jnp.int32) for t in range(n_band // tile)],
        axis=1,
    )
    stack = 4 * rel_count
    id_rows = lax.broadcasted_iota(jnp.int32, (stack, n_all), 0) % rel_count
    rel_hot = jnp.where(id_rows == ids, 1.0, 0.0).astype(bf16)
    w = weights[...]
    w_1 = w.astype(bf16).astype(f32)
    w_2 = (w - w_1).astype(bf16).astype(f32)
    w_3 = w - w_1 - w_2
    w_stack = jnp.concatenate([w_1, w_2, w_3, jnp.zeros_like(w)], axis=0).astype(bf16)
    w_t = tn(w_stack, rel_hot)
    q = (rows_t * w_t).astype(bf16)
    q_f = q.astype(f32)
    q_all[pl.ds(0, width), :] = q
    if padded > width:
        rest = pl.ds(width, padded - width)
        q_all[rest, :] = jnp.zeros((padded - width, n_all), bf16)
        dt_all[rest, :] = jnp.zeros((padded - width, n_edge), bf16)
        lo_keep[rest, :] = jnp.zeros((padded - width, rows), f32)
        lo_out[rest, :] = jnp.zeros((padded - width, rows), bf16)
    dst_hot = hot(dst[...], rows)
    bdst_hot = hot(bdst[...], rows)
    edge_ids = lax.broadcasted_iota(jnp.int32, (1, n_all), 1)
    limit = live_ref[0, 0] * tile
    valid = jnp.where((edge_ids < limit) | (edge_ids >= n_edge), 1.0, 0.0)
    row_tile = lax.broadcasted_iota(jnp.int32, (rows, 1), 0) // tile
    counts = jnp.zeros((rows, 1), f32)
    for k in range(n_neg):
        counts = counts + jnp.where(row_tile == neg_ids[0, k], 1.0, 0.0)
    scale = (counts * (0.5 / (n_neg * tile))) * valid

    def edge_pos(edges, target_t, weight):
        pos = jnp.sum(q_f[:, edges] * target_t, axis=0, keepdims=True)
        dpos = -weight / (1.0 + jnp.exp(pos))
        return dpos, (dpos * q_f[:, edges]).astype(bf16)

    near_there = near.at[:, lanes(1 - core)]
    near_mate = remote(near_there, near_there, s_mate.at[0], r_mate.at[0], (dom, mate))

    @pl.when(hears_near == 1)
    def _():
        near_copy.wait_recv()
        near_mate.start()

    for step in range(len(route)):
        out_copy.wait()
        if direct:
            break
        moved = routed(far_step, own_half, step).astype(bf16)
        if step < len(route) - 1:
            far_step[2 * step + 2] = moved
            out_copy = route_copy(far_step, own_half, step + 1, s_route, r_route, far_half)
            out_copy.start()
        else:
            far_half[...] = moved
    far_copy = remote(far_half, far_half, s_far.at[0], r_far.at[0], (dom, mate))
    far_copy.start()

    @pl.when(sends_near == 1)
    def _():
        near_copy.wait_send()
        near_mate.wait_recv()

    @pl.when(hears_near == 1)
    def _():
        near_mate.wait_send()

    near_t = nn(near[...], bdst_hot)
    band_dpos, band_dtarget = edge_pos(slice(n_edge, n_all), near_t, jnp.ones((1, n_band), f32))
    near_out[...] = nt(band_dtarget, bdst_hot).astype(bf16)
    pair_copy = remote(
        near_out.at[:, lanes(1 - core)], pair_in, s_pair.at[0], r_pair.at[0], (dom, mate)
    )
    pair_copy.start()
    band_dq = band_dpos * near_t
    far_copy.wait()

    far_t = far[...]
    target_t = nn(far_t, dst_hot)
    dpos, dtarget = edge_pos(slice(0, n_edge), target_t, valid[:, :n_edge])
    dt_all[pl.ds(0, width), :] = dtarget

    pair_copy.wait()
    near_sum[...] = (near_out[:, lanes(core)].astype(f32) + pair_in[...].astype(f32)).astype(bf16)
    back_near = remote(near_sum, near_back, s_nback.at[0], r_nback.at[0], (beside, rel))

    @pl.when(sends_near == 1)
    def _():
        back_near.start()

    neg = tn(far_t, q)
    dneg = (scale + scale * jnp.tanh(0.5 * neg)).astype(bf16)

    def block_copy(source, target, slot, sends, recvs, peer):
        block = source.at[down(peer // 2), lanes(peer % 2)]
        return remote(block, target.at[slot], sends.at[slot], recvs.at[slot], (dom, peer))

    def group(k):
        y_k = (y + 1 + k) % n_y
        if k == n_y - 1:
            return [(2 * k, mate)]
        return [(2 * k, y_k * 2 + core), (2 * k + 1, y_k * 2 + 1 - core)]

    fg_copies = []
    for k in range(n_y):
        band = down((y + 1 + k) % n_y)
        far_grad = nt(dt_all[band, :], dst_hot) + nt(q_all[band, :], dneg)
        fg_out[band, :] = far_grad.astype(bf16)
        if k == n_y - 1:
            fg_keep[...] = far_grad
        for slot, peer in group(k):
            copy = block_copy(fg_out, fg_in, slot, s_fg, r_fg, peer)
            copy.start()
            fg_copies.append(copy)

    dq = jnp.concatenate([dpos * target_t, band_dq], axis=1) + nn(far_t, dneg)
    own_grad = nt((dq * w_t).astype(bf16), src_hot)

    @pl.when(hears_near == 1)
    def _():
        back_near.wait_recv()

    @pl.when(sends_near == 1)
    def _():
        back_near.wait_send()

    heard_hot = hot(bound[:, lanes(1 - core)], rows)
    local_grad = own_grad + nt(near_back[...], heard_hot)
    lo_keep[pl.ds(0, width), :] = local_grad
    lo_out[pl.ds(0, width), :] = local_grad.astype(bf16)
    lo_copies = []
    for k in range(n_y):
        for slot, peer in group(k):
            copy = block_copy(lo_out, lo_in, slot, s_lo, r_lo, peer)
            copy.start()
            lo_copies.append(copy)

    def gw_copy(level):
        return remote(
            gw_out.at[level],
            gw_in.at[level],
            s_gw.at[level],
            r_gw.at[level],
            (flipped(dom, levels[level]), rel),
        )

    def gw_step(level):
        gw_copy(level).wait()
        total = gw_out[level] + gw_in[level]
        if level < len(levels) - 1:
            gw_out[level + 1] = total
            gw_copy(level + 1).start()
        return total

    gw_out[0] = nt(rel_hot, (dq * rows_t).astype(bf16))[:rel_count]
    gw_copy(0).start()

    for copy in fg_copies:
        copy.wait()
    total = fg_keep[:, lanes(core)]
    for k in range(n_rel - 1):
        total = total + fg_in[k].astype(f32)
    back[0] = total.astype(bf16)
    back_copy = route_copy(back, back.at[0], 0, s_back, r_back, back.at[1])
    back_copy.start()

    gw = gw_step(0)
    for copy in lo_copies:
        copy.wait()
    local = lo_keep[down(y), lanes(core)]
    for k in range(n_rel - 1):
        local = local + lo_in[k].astype(f32)

    for step in range(len(route)):
        back_copy.wait()
        if direct:
            total = back[1].astype(f32)
            break
        total = routed(back, back.at[0], step)
        if step < len(route) - 1:
            back[2 * step + 2] = total.astype(bf16)
            back_copy = route_copy(back, back.at[0], step + 1, s_back, r_back, None)
            back_copy.start()
    g_block = g_all.at[down(y), lanes(core)]
    g_block[...] = (local + total).astype(bf16)
    g_copies = [
        remote(g_block, g_block, s_g.at[k], r_g.at[k], (dom, peer))
        for k, peer in enumerate(peers)
    ]
    for copy in g_copies:
        copy.start()

    for level in range(1, len(levels)):
        gw = gw_step(level)
    eye_rel = lax.broadcasted_iota(jnp.int32, (rel_count, rel_count), 0) == (
        lax.broadcasted_iota(jnp.int32, (rel_count, rel_count), 1)
    )
    rel_col = jnp.sum(jnp.where(eye_rel, rel_state[...], 0.0), axis=1, keepdims=True)
    rel_fresh = rel_col + jnp.mean(gw * gw, axis=1, keepdims=True)
    rel_out[...] = weights[...] - step_rate * gw / jnp.sqrt(rel_fresh)

    for copy in g_copies:
        copy.wait()
    grad_t = g_all[pl.ds(0, width), :].astype(f32)
    fresh = state[...] + jnp.sum(grad_t * grad_t, axis=0, keepdims=True) * (1.0 / width)
    state_out[...] = fresh
    emb_out[...] = emb_t[...] - grad_t * (step_rate / jnp.sqrt(fresh))


def updates(n_dom, n_rel, route, collective_id, args):
    emb_t, weights = args[5], args[7]
    width, rows = emb_t.shape
    rel_count = weights.shape[0]
    n_y = n_rel // 2
    padded = pl.cdiv(width, 16 * n_y) * 16 * n_y
    part = padded // n_y
    half = rows // 2
    edges = args[9].shape[1]
    band = args[12].shape[1]
    peers = n_rel - 1
    levels = n_dom.bit_length() - 1
    steps = len(route)
    table = pltpu.VMEM((width, rows), bf16)
    side = pltpu.VMEM((width, half), bf16)
    tall = pltpu.VMEM((padded, rows), bf16)
    blocks = pltpu.VMEM((peers, part, half), bf16)
    one = pltpu.SemaphoreType.DMA((1,))
    to_peers = pltpu.SemaphoreType.DMA((peers,))
    per_step = pltpu.SemaphoreType.DMA((steps,))
    per_level = pltpu.SemaphoreType.DMA((levels,))
    small = pltpu.VMEM((levels, rel_count, width), f32)
    smem = pl.BlockSpec(memory_space=pltpu.SMEM)
    vmem = pl.BlockSpec(memory_space=pltpu.VMEM)
    semaphores = [per_step, one, one, one, one, one, to_peers, to_peers, per_step, to_peers]
    semaphores = [kind for kind in semaphores + [per_level] for _ in range(2)]
    return pl.pallas_call(
        functools.partial(kernel, n_dom, n_rel, route),
        out_shape=(
            jax.ShapeDtypeStruct((width, rows), f32),
            jax.ShapeDtypeStruct((1, rows), f32),
            jax.ShapeDtypeStruct((rel_count, width), f32),
        ),
        in_specs=[smem] * 5 + [vmem] * 9,
        out_specs=(vmem, vmem, vmem),
        scratch_shapes=[
            table,
            table,
            pltpu.VMEM((2 * steps, width, half), bf16),
            table,
            table,
            table,
            side,
            side,
            side,
            pltpu.VMEM((part, rows), f32),
            tall,
            blocks,
            pltpu.VMEM((padded, rows), f32),
            tall,
            blocks,
            pltpu.VMEM((2 * steps, part, half), bf16),
            tall,
            pltpu.VMEM((padded, edges + band), bf16),
            pltpu.VMEM((padded, edges), bf16),
            small,
            small,
        ]
        + semaphores,
        compiler_params=pltpu.CompilerParams(
            collective_id=collective_id,
            has_side_effects=True,
            vmem_limit_bytes=48 * 1024 * 1024,
        ),
    )(*args)


def body(
    emb,
    emb_state,
    rel_weight,
    rel_state,
    swap_mask,
    src_rows,
    dst_rows,
    tile_rel,
    live_tiles,
    neg_tiles,
    bound_rows,
    band_src,
    band_dst,
    band_rel,
):
    n_dom = lax.axis_size("dom")
    n_rel = lax.axis_size("rel")
    args = (
        swap_mask,
        tile_rel,
        live_tiles,
        neg_tiles,
        band_rel,
        emb.T,
        emb_state.reshape(1, -1),
        rel_weight,
        rel_state.reshape(1, -1),
        src_rows,
        dst_rows,
        bound_rows.reshape(1, -1),
        band_src,
        band_dst,
    )
    if n_dom <= 8:
        branches = [
            functools.partial(updates, n_dom, n_rel, [(m, None)], m) for m in range(1, n_dom)
        ]
        emb_t, state_new, rel_new = lax.switch(swap_mask[0] - 1, branches, args)
    else:
        route = [(1 << bit, bit) for bit in range(n_dom.bit_length() - 1)]
        emb_t, state_new, rel_new = updates(n_dom, n_rel, route, 0, args)
    return (emb_t.T, state_new.reshape(-1), rel_new)


def solution(mesh):
    in_specs = (
        P("dom", None),
        P("dom"),
        P("rel", None),
        P("rel"),
        P(),
        P("rel", "dom"),
        P("rel", "dom"),
        P("rel", "dom"),
        P("rel", "dom"),
        P("rel", "dom"),
        P("dom"),
        P("rel", "dom"),
        P("rel", "dom"),
        P("rel", "dom"),
    )
    out_specs = (P("dom", None), P("dom"), P("rel", None))
    return jax.shard_map(body, mesh=mesh, in_specs=in_specs, out_specs=out_specs, check_vma=False)
```

```python
import functools

import jax
import jax.numpy as jnp
from jax import lax
from jax.experimental import pallas as pl
from jax.experimental.pallas import tpu as pltpu
from jax.sharding import PartitionSpec as P

step_rate = 0.25
tile = 128
MESH = pl.DeviceIdType.MESH
f32 = jnp.float32
bf16 = jnp.bfloat16


def dot(a, b, dims):
    return lax.dot_general(a, b, (dims, ((), ())), preferred_element_type=f32)


def nn(a, b):
    return dot(a, b, ((1,), (0,)))


def nt(a, b):
    return dot(a, b, ((1,), (1,)))


def tn(a, b):
    return dot(a, b, ((0,), (0,)))


def flipped(index, distance):
    bit = 1
    out = index
    while bit <= distance:
        if distance & bit:
            out = out + bit * (1 - 2 * ((index // bit) % 2))
        bit *= 2
    return out


def hot(ids, count):
    rows = lax.broadcasted_iota(jnp.int32, (count, ids.shape[1]), 0)
    return jnp.where(rows == ids, 1.0, 0.0).astype(bf16)


def kernel(
    n_dom,
    n_rel,
    route,
    mask_h,
    tile_rel_h,
    live_h,
    neg_ids_h,
    band_rel_h,
    emb_h,
    state_h,
    weights_h,
    rel_state_h,
    src_h,
    dst_h,
    bound_h,
    bsrc_h,
    bdst_h,
    emb_out,
    state_out,
    rel_out,
    own,
    far,
    far_step,
    rim,
    near,
    near_out,
    pair_in,
    near_sum,
    near_back,
    fg_keep,
    fg_out,
    fg_in,
    lo_keep,
    lo_out,
    lo_in,
    back,
    g_all,
    q_all,
    dt_all,
    gw_out,
    gw_in,
    mask_ref,
    tile_rel,
    live_ref,
    neg_ids,
    band_rel,
    emb_t,
    state,
    weights,
    rel_state,
    src_all,
    dst,
    bound,
    bdst,
    low_part,
    w_stack,
    rel_hot,
    src_hot,
    dst_hot,
    rows_t,
    w_t,
    push,
    far_rows,
    dneg,
    dqw,
    dqr,
    valid,
    s_in,
    s_route,
    r_route,
    s_far,
    r_far,
    s_near,
    r_near,
    s_mate,
    r_mate,
    s_pair,
    r_pair,
    s_nback,
    r_nback,
    s_fg,
    r_fg,
    s_lo,
    r_lo,
    s_back,
    r_back,
    s_g,
    r_g,
    s_gw,
    r_gw,
):
    width, rows = emb_t.shape
    half = rows // 2
    n_y = n_rel // 2
    padded = g_all.shape[0]
    part = padded // n_y
    rel_count = weights.shape[0]
    n_edge = dst.shape[1]
    n_band = bdst.shape[1]
    n_all = n_edge + n_band
    n_neg = neg_ids.shape[1]
    dom = lax.axis_index("dom")
    rel = lax.axis_index("rel")
    y = rel // 2
    core = rel % 2
    mate = rel + 1 - 2 * core
    levels = [1 << b for b in range(n_dom.bit_length() - 1)]
    partners = sorted(set(levels) | {distance for distance, _ in route})
    direct = route[0][1] is None
    has_low = (dom + n_dom - 1) // n_dom
    has_high = 1 - dom // (n_dom - 1)
    sends_near = core * has_high + (1 - core) * has_low
    hears_near = core * has_low + (1 - core) * has_high
    beside = dom + 2 * core - 1
    peers = [lax.rem(rel + k, n_rel) for k in range(1, n_rel)]

    def lanes(which):
        return pl.ds(pl.multiple_of(which * half, half), half)

    def down(which):
        return pl.ds(pl.multiple_of(which * part, part), part)

    block = 2 * tile if n_edge % (2 * tile) == 0 and n_band % (2 * tile) == 0 else tile

    def cols(index):
        return pl.ds(pl.multiple_of(index * block, block), block)

    def over(first, last, step):
        def one(index, carry):
            step(cols(index))
            return carry

        lax.fori_loop(first // block, last // block, one, 0)

    pairs = [
        (emb_h, emb_t),
        (bound_h, bound),
        (src_h, src_all.at[:, pl.ds(0, n_edge)]),
        (bsrc_h, src_all.at[:, pl.ds(n_edge, n_band)]),
        (weights_h, weights),
        (tile_rel_h, tile_rel),
        (band_rel_h, band_rel),
        (dst_h, dst),
        (bdst_h, bdst),
        (live_h, live_ref),
        (neg_ids_h, neg_ids),
        (state_h, state),
        (rel_state_h, rel_state),
        (mask_h, mask_ref),
    ]
    loads = [pltpu.make_async_copy(a, b, s_in.at[k]) for k, (a, b) in enumerate(pairs)]
    for load in loads:
        load.start()
    near_back[...] = jnp.zeros_like(near_back)
    near[...] = jnp.zeros_like(near)

    barrier = pltpu.get_barrier_semaphore()
    for peer in peers:
        pl.semaphore_signal(barrier, inc=1, device_id=(dom, peer), device_id_type=MESH)
    for distance in partners:
        pl.semaphore_signal(
            barrier, inc=1, device_id=(flipped(dom, distance), rel), device_id_type=MESH
        )

    @pl.when(has_low == 1)
    def _():
        pl.semaphore_signal(barrier, inc=1, device_id=(dom - 1, rel), device_id_type=MESH)

    @pl.when(has_high == 1)
    def _():
        pl.semaphore_signal(barrier, inc=1, device_id=(dom + 1, rel), device_id_type=MESH)

    loads[0].wait()
    table = emb_t[...]
    own_t = table.astype(bf16)
    own[...] = own_t
    low_part[...] = (table - own_t.astype(f32)).astype(bf16)
    pl.semaphore_wait(barrier, len(peers) + len(partners) + has_low + has_high)

    def remote(source, target, send, recv, device):
        return pltpu.make_async_remote_copy(
            src_ref=source,
            dst_ref=target,
            send_sem=send,
            recv_sem=recv,
            device_id=device,
            device_id_type=MESH,
        )

    def route_copy(buffer, first, step, sends, recvs, last):
        distance, _ = route[step]
        return remote(
            first if step == 0 else buffer.at[2 * step],
            last if direct else buffer.at[2 * step + 1],
            sends.at[step],
            recvs.at[step],
            (flipped(dom, distance), rel),
        )

    def routed(buffer, first, step):
        got = buffer[2 * step + 1].astype(f32)
        held = (first[...] if step == 0 else buffer[2 * step]).astype(f32)
        moved = (mask_ref[0] // (1 << route[step][1])) % 2
        return jnp.where(moved == 1, got, held)

    own_half = own.at[:, lanes(core)]
    far_half = far.at[:, lanes(core)]
    out_copy = route_copy(far_step, own_half, 0, s_route, r_route, far_half)
    out_copy.start()

    for load in loads[1:]:
        load.wait()
    bound_hot = hot(bound[...], rows)
    rim[...] = nn(own_t, bound_hot).astype(bf16)
    near_copy = remote(
        rim.at[:, lanes(core)], near.at[:, lanes(1 - core)], s_near.at[0], r_near.at[0], (beside, rel)
    )

    @pl.when(sends_near == 1)
    def _():
        near_copy.start()

    ids = jnp.concatenate(
        [jnp.full((1, tile), tile_rel[0, t], jnp.int32) for t in range(n_edge // tile)]
        + [jnp.full((1, tile), band_rel[0, t], jnp.int32) for t in range(n_band // tile)],
        axis=1,
    )
    stack = 4 * rel_count
    id_rows = lax.broadcasted_iota(jnp.int32, (stack, n_all), 0) % rel_count
    rel_hot[...] = jnp.where(id_rows == ids, 1.0, 0.0).astype(bf16)
    w = weights[...]
    w_1 = w.astype(bf16).astype(f32)
    w_2 = (w - w_1).astype(bf16).astype(f32)
    w_3 = w - w_1 - w_2
    w_stack[...] = jnp.concatenate([w_1, w_2, w_3, jnp.zeros_like(w)], axis=0).astype(bf16)
    inner = pl.ds(0, width)

    def edge_rows(at):
        hot_here = hot(src_all[:, at], rows)
        rows_here = nn(own[...], hot_here) + nn(low_part[...], hot_here)
        w_here = tn(w_stack[...], rel_hot[:, at])
        src_hot[:, at] = hot_here
        rows_t[:, at] = rows_here
        w_t[:, at] = w_here
        q_all[inner, at] = (rows_here * w_here).astype(bf16)

    over(0, n_all, edge_rows)

    def target_hot(at):
        dst_hot[:, at] = hot(dst[:, at], rows)

    over(0, n_edge, target_hot)
    if padded > width:
        rest = pl.ds(width, padded - width)
        q_all[rest, :] = jnp.zeros((padded - width, n_all), bf16)
        dt_all[rest, :] = jnp.zeros((padded - width, n_edge), bf16)
        lo_keep[rest, :] = jnp.zeros((padded - width, rows), f32)
        lo_out[rest, :] = jnp.zeros((padded - width, rows), bf16)
    bdst_hot = hot(bdst[...], rows)
    edge_ids = lax.broadcasted_iota(jnp.int32, (1, n_all), 1)
    limit = live_ref[0, 0] * tile
    valid[...] = jnp.where((edge_ids < limit) | (edge_ids >= n_edge), 1.0, 0.0)
    row_tile = lax.broadcasted_iota(jnp.int32, (rows, 1), 0) // tile
    counts = jnp.zeros((rows, 1), f32)
    for k in range(n_neg):
        counts = counts + jnp.where(row_tile == neg_ids[0, k], 1.0, 0.0)
    scale = counts * (0.5 / (n_neg * tile))

    def edge_pos(at, target_t, weight):
        q_here = q_all[inner, at].astype(f32)
        pos = jnp.sum(q_here * target_t, axis=0, keepdims=True)
        dpos = -weight / (1.0 + jnp.exp(pos))
        push[:, at] = dpos * target_t
        return (dpos * q_here).astype(bf16)

    near_there = near.at[:, lanes(1 - core)]
    near_mate = remote(near_there, near_there, s_mate.at[0], r_mate.at[0], (dom, mate))

    @pl.when(hears_near == 1)
    def _():
        near_copy.wait_recv()
        near_mate.start()

    for step in range(len(route)):
        out_copy.wait()
        if direct:
            break
        moved = routed(far_step, own_half, step).astype(bf16)
        if step < len(route) - 1:
            far_step[2 * step + 2] = moved
            out_copy = route_copy(far_step, own_half, step + 1, s_route, r_route, far_half)
            out_copy.start()
        else:
            far_half[...] = moved
    far_copy = remote(far_half, far_half, s_far.at[0], r_far.at[0], (dom, mate))
    far_copy.start()

    @pl.when(sends_near == 1)
    def _():
        near_copy.wait_send()
        near_mate.wait_recv()

    @pl.when(hears_near == 1)
    def _():
        near_mate.wait_send()

    band_dtarget = edge_pos(
        pl.ds(n_edge, n_band), nn(near[...], bdst_hot), jnp.ones((1, n_band), f32)
    )
    near_out[...] = nt(band_dtarget, bdst_hot).astype(bf16)
    pair_copy = remote(
        near_out.at[:, lanes(1 - core)], pair_in, s_pair.at[0], r_pair.at[0], (dom, mate)
    )
    pair_copy.start()
    far_copy.wait()

    def edge_targets(at):
        dt_all[inner, at] = edge_pos(at, nn(far[...], dst_hot[:, at]), valid[:, at])

    over(0, n_edge, edge_targets)
    pair_copy.wait()
    near_sum[...] = (near_out[:, lanes(core)].astype(f32) + pair_in[...].astype(f32)).astype(bf16)
    back_near = remote(near_sum, near_back, s_nback.at[0], r_nback.at[0], (beside, rel))

    @pl.when(sends_near == 1)
    def _():
        back_near.start()

    far_rows[...] = far[...].T

    def edge_negs(at):
        neg = nn(far_rows[...], q_all[inner, at])
        weight = scale * valid[:, at]
        dneg[:, at] = (weight + weight * jnp.tanh(0.5 * neg)).astype(bf16)

    over(0, n_all, edge_negs)

    def block_copy(source, target, slot, sends, recvs, peer):
        block = source.at[down(peer // 2), lanes(peer % 2)]
        return remote(block, target.at[slot], sends.at[slot], recvs.at[slot], (dom, peer))

    def group(k):
        y_k = (y + 1 + k) % n_y
        if k == n_y - 1:
            return [(2 * k, mate)]
        return [(2 * k, y_k * 2 + core), (2 * k + 1, y_k * 2 + 1 - core)]

    fg_copies = []
    for k in range(n_y):
        band = down((y + 1 + k) % n_y)
        far_grad = nt(dt_all[band, :], dst_hot[...]) + nt(q_all[band, :], dneg[...])
        fg_out[band, :] = far_grad.astype(bf16)
        if k == n_y - 1:
            fg_keep[...] = far_grad
        for slot, peer in group(k):
            copy = block_copy(fg_out, fg_in, slot, s_fg, r_fg, peer)
            copy.start()
            fg_copies.append(copy)

    def edge_sources(at):
        dq = push[:, at] + nn(far[...], dneg[:, at])
        dqw[:, at] = (dq * w_t[:, at]).astype(bf16)
        dqr[:, at] = (dq * rows_t[:, at]).astype(bf16)

    over(0, n_all, edge_sources)
    own_grad = nt(dqw[...], src_hot[...])

    @pl.when(hears_near == 1)
    def _():
        back_near.wait_recv()

    @pl.when(sends_near == 1)
    def _():
        back_near.wait_send()

    heard_hot = hot(bound[:, lanes(1 - core)], rows)
    local_grad = own_grad + nt(near_back[...], heard_hot)
    lo_keep[pl.ds(0, width), :] = local_grad
    lo_out[pl.ds(0, width), :] = local_grad.astype(bf16)
    lo_copies = []
    for k in range(n_y):
        for slot, peer in group(k):
            copy = block_copy(lo_out, lo_in, slot, s_lo, r_lo, peer)
            copy.start()
            lo_copies.append(copy)

    def gw_copy(level):
        return remote(
            gw_out.at[level],
            gw_in.at[level],
            s_gw.at[level],
            r_gw.at[level],
            (flipped(dom, levels[level]), rel),
        )

    def gw_step(level):
        gw_copy(level).wait()
        total = gw_out[level] + gw_in[level]
        if level < len(levels) - 1:
            gw_out[level + 1] = total
            gw_copy(level + 1).start()
        return total

    gw_out[0] = nt(rel_hot[...], dqr[...])[:rel_count]
    gw_copy(0).start()

    for copy in fg_copies:
        copy.wait()
    total = fg_keep[:, lanes(core)]
    for k in range(n_rel - 1):
        total = total + fg_in[k].astype(f32)
    back[0] = total.astype(bf16)
    back_copy = route_copy(back, back.at[0], 0, s_back, r_back, back.at[1])
    back_copy.start()

    gw = gw_step(0)
    for copy in lo_copies:
        copy.wait()
    local = lo_keep[down(y), lanes(core)]
    for k in range(n_rel - 1):
        local = local + lo_in[k].astype(f32)

    for step in range(len(route)):
        back_copy.wait()
        if direct:
            total = back[1].astype(f32)
            break
        total = routed(back, back.at[0], step)
        if step < len(route) - 1:
            back[2 * step + 2] = total.astype(bf16)
            back_copy = route_copy(back, back.at[0], step + 1, s_back, r_back, None)
            back_copy.start()
    g_block = g_all.at[down(y), lanes(core)]
    g_block[...] = (local + total).astype(bf16)
    g_copies = [
        remote(g_block, g_block, s_g.at[k], r_g.at[k], (dom, peer))
        for k, peer in enumerate(peers)
    ]
    for copy in g_copies:
        copy.start()

    for level in range(1, len(levels)):
        gw = gw_step(level)
    eye_rel = lax.broadcasted_iota(jnp.int32, (rel_count, rel_count), 0) == (
        lax.broadcasted_iota(jnp.int32, (rel_count, rel_count), 1)
    )
    rel_col = jnp.sum(jnp.where(eye_rel, rel_state[...], 0.0), axis=1, keepdims=True)
    rel_fresh = rel_col + jnp.mean(gw * gw, axis=1, keepdims=True)
    rel_out[...] = weights[...] - step_rate * gw / jnp.sqrt(rel_fresh)

    for copy in g_copies:
        copy.wait()
    grad_t = g_all[pl.ds(0, width), :].astype(f32)
    fresh = state[...] + jnp.sum(grad_t * grad_t, axis=0, keepdims=True) * (1.0 / width)
    state_out[...] = fresh
    emb_out[...] = emb_t[...] - grad_t * (step_rate / jnp.sqrt(fresh))


def updates(n_dom, n_rel, route, collective_id, args):
    emb_t, weights = args[5], args[7]
    width, rows = emb_t.shape
    rel_count = weights.shape[0]
    n_y = n_rel // 2
    padded = pl.cdiv(width, 16 * n_y) * 16 * n_y
    part = padded // n_y
    half = rows // 2
    edges = args[9].shape[1]
    band = args[12].shape[1]
    peers = n_rel - 1
    levels = n_dom.bit_length() - 1
    steps = len(route)
    table = pltpu.VMEM((width, rows), bf16)
    side = pltpu.VMEM((width, half), bf16)
    tall = pltpu.VMEM((padded, rows), bf16)
    blocks = pltpu.VMEM((peers, part, half), bf16)
    one = pltpu.SemaphoreType.DMA((1,))
    to_peers = pltpu.SemaphoreType.DMA((peers,))
    per_step = pltpu.SemaphoreType.DMA((steps,))
    per_level = pltpu.SemaphoreType.DMA((levels,))
    small = pltpu.VMEM((levels, rel_count, width), f32)
    hbm = pl.BlockSpec(memory_space=pltpu.HBM)
    vmem = pl.BlockSpec(memory_space=pltpu.VMEM)
    semaphores = [per_step, one, one, one, one, one, to_peers, to_peers, per_step, to_peers]
    semaphores = [kind for kind in semaphores + [per_level] for _ in range(2)]
    return pl.pallas_call(
        functools.partial(kernel, n_dom, n_rel, route),
        out_shape=(
            jax.ShapeDtypeStruct((width, rows), f32),
            jax.ShapeDtypeStruct((1, rows), f32),
            jax.ShapeDtypeStruct((rel_count, width), f32),
        ),
        in_specs=[hbm] * len(args),
        out_specs=(vmem, vmem, vmem),
        scratch_shapes=[
            table,
            table,
            pltpu.VMEM((2 * steps, width, half), bf16),
            table,
            table,
            table,
            side,
            side,
            side,
            pltpu.VMEM((part, rows), f32),
            tall,
            blocks,
            pltpu.VMEM((padded, rows), f32),
            tall,
            blocks,
            pltpu.VMEM((2 * steps, part, half), bf16),
            tall,
            pltpu.VMEM((padded, edges + band), bf16),
            pltpu.VMEM((padded, edges), bf16),
            small,
            small,
            *[pltpu.SMEM(arg.shape, arg.dtype) for arg in args[:5]],
            *[pltpu.VMEM(arg.shape, arg.dtype) for arg in args[5:9]],
            pltpu.VMEM((1, edges + band), jnp.int32),
            pltpu.VMEM((1, edges), jnp.int32),
            pltpu.VMEM((1, rows), jnp.int32),
            pltpu.VMEM((1, band), jnp.int32),
            table,
            pltpu.VMEM((4 * rel_count, width), bf16),
            pltpu.VMEM((4 * rel_count, edges + band), bf16),
            pltpu.VMEM((rows, edges + band), bf16),
            pltpu.VMEM((rows, edges), bf16),
            pltpu.VMEM((width, edges + band), f32),
            pltpu.VMEM((width, edges + band), f32),
            pltpu.VMEM((width, edges + band), f32),
            pltpu.VMEM((rows, width), bf16),
            pltpu.VMEM((rows, edges + band), bf16),
            pltpu.VMEM((width, edges + band), bf16),
            pltpu.VMEM((width, edges + band), bf16),
            pltpu.VMEM((1, edges + band), f32),
            pltpu.SemaphoreType.DMA((len(args),)),
        ]
        + semaphores,
        compiler_params=pltpu.CompilerParams(
            collective_id=collective_id,
            has_side_effects=True,
            vmem_limit_bytes=48 * 1024 * 1024,
        ),
    )(*args)


def body(
    emb,
    emb_state,
    rel_weight,
    rel_state,
    swap_mask,
    src_rows,
    dst_rows,
    tile_rel,
    live_tiles,
    neg_tiles,
    bound_rows,
    band_src,
    band_dst,
    band_rel,
):
    n_dom = lax.axis_size("dom")
    n_rel = lax.axis_size("rel")
    args = (
        swap_mask,
        tile_rel,
        live_tiles,
        neg_tiles,
        band_rel,
        emb.T,
        emb_state.reshape(1, -1),
        rel_weight,
        rel_state.reshape(1, -1),
        src_rows,
        dst_rows,
        bound_rows.reshape(1, -1),
        band_src,
        band_dst,
    )
    if n_dom <= 8:
        branches = [
            functools.partial(updates, n_dom, n_rel, [(m, None)], m) for m in range(1, n_dom)
        ]
        emb_t, state_new, rel_new = lax.switch(swap_mask[0] - 1, branches, args)
    else:
        route = [(1 << bit, bit) for bit in range(n_dom.bit_length() - 1)]
        emb_t, state_new, rel_new = updates(n_dom, n_rel, route, 0, args)
    return (emb_t.T, state_new.reshape(-1), rel_new)


def solution(mesh):
    in_specs = (
        P("dom", None),
        P("dom"),
        P("rel", None),
        P("rel"),
        P(),
        P("rel", "dom"),
        P("rel", "dom"),
        P("rel", "dom"),
        P("rel", "dom"),
        P("rel", "dom"),
        P("dom"),
        P("rel", "dom"),
        P("rel", "dom"),
        P("rel", "dom"),
    )
    out_specs = (P("dom", None), P("dom"), P("rel", None))
    return jax.shard_map(body, mesh=mesh, in_specs=in_specs, out_specs=out_specs, check_vma=False)
```

```python
import functools

import jax
import jax.numpy as jnp
from jax import lax
from jax.experimental import pallas as pl
from jax.experimental.pallas import tpu as pltpu
from jax.sharding import PartitionSpec as P

step_rate = 0.25
tile = 128
MESH = pl.DeviceIdType.MESH
f32 = jnp.float32
bf16 = jnp.bfloat16


def dot(a, b, dims):
    return lax.dot_general(a, b, (dims, ((), ())), preferred_element_type=f32)


def nn(a, b):
    return dot(a, b, ((1,), (0,)))


def nt(a, b):
    return dot(a, b, ((1,), (1,)))


def tn(a, b):
    return dot(a, b, ((0,), (0,)))


def flipped(index, distance):
    bit = 1
    out = index
    while bit <= distance:
        if distance & bit:
            out = out + bit * (1 - 2 * ((index // bit) % 2))
        bit *= 2
    return out


def hot(ids, count):
    rows = lax.broadcasted_iota(jnp.int32, (count, ids.shape[1]), 0)
    return jnp.where(rows == ids, 1.0, 0.0).astype(bf16)


def kernel(
    n_dom,
    n_rel,
    route,
    mask_h,
    tile_rel_h,
    live_h,
    neg_ids_h,
    band_rel_h,
    emb_h,
    state_h,
    weights_h,
    rel_state_h,
    src_h,
    dst_h,
    bound_h,
    bsrc_h,
    bdst_h,
    emb_out,
    state_out,
    rel_out,
    own,
    far,
    far_step,
    rim,
    near,
    near_out,
    pair_in,
    near_sum,
    near_back,
    fg_keep,
    fg_out,
    fg_in,
    lo_keep,
    lo_out,
    lo_in,
    back,
    g_all,
    q_all,
    dt_all,
    gw_out,
    gw_in,
    mask_ref,
    tile_rel,
    live_ref,
    neg_ids,
    band_rel,
    emb_t,
    state,
    weights,
    rel_state,
    src_all,
    dst,
    bound,
    bdst,
    low_part,
    w_stack,
    rel_hot,
    src_hot,
    dst_hot,
    rows_t,
    w_t,
    push,
    far_rows,
    dneg,
    dqw,
    dqr,
    valid,
    s_in,
    s_route,
    r_route,
    s_far,
    r_far,
    s_near,
    r_near,
    s_mate,
    r_mate,
    s_pair,
    r_pair,
    s_nback,
    r_nback,
    s_fg,
    r_fg,
    s_lo,
    r_lo,
    s_back,
    r_back,
    s_g,
    r_g,
    s_gw,
    r_gw,
):
    width, rows = emb_t.shape
    half = rows // 2
    n_y = n_rel // 2
    padded = g_all.shape[0]
    part = padded // n_y
    rel_count = weights.shape[0]
    n_edge = dst.shape[1]
    n_band = bdst.shape[1]
    n_all = n_edge + n_band
    n_neg = neg_ids.shape[1]
    dom = lax.axis_index("dom")
    rel = lax.axis_index("rel")
    y = rel // 2
    core = rel % 2
    mate = rel + 1 - 2 * core
    levels = [1 << b for b in range(n_dom.bit_length() - 1)]
    partners = sorted(set(levels) | {distance for distance, _ in route})
    direct = route[0][1] is None
    has_low = (dom + n_dom - 1) // n_dom
    has_high = 1 - dom // (n_dom - 1)
    sends_near = core * has_high + (1 - core) * has_low
    hears_near = core * has_low + (1 - core) * has_high
    beside = dom + 2 * core - 1
    peers = [lax.rem(rel + k, n_rel) for k in range(1, n_rel)]

    def lanes(which):
        return pl.ds(pl.multiple_of(which * half, half), half)

    def down(which):
        return pl.ds(pl.multiple_of(which * part, part), part)

    block = 2 * tile if n_edge % (2 * tile) == 0 and n_band % (2 * tile) == 0 else tile

    def cols(index):
        return pl.ds(pl.multiple_of(index * block, block), block)

    def over(first, last, step):
        def one(index, carry):
            step(cols(index))
            return carry

        lax.fori_loop(first // block, last // block, one, 0)

    pairs = [
        (emb_h, emb_t),
        (bound_h, bound),
        (src_h, src_all.at[:, pl.ds(0, n_edge)]),
        (bsrc_h, src_all.at[:, pl.ds(n_edge, n_band)]),
        (weights_h, weights),
        (tile_rel_h, tile_rel),
        (band_rel_h, band_rel),
        (dst_h, dst),
        (bdst_h, bdst),
        (live_h, live_ref),
        (neg_ids_h, neg_ids),
        (state_h, state),
        (rel_state_h, rel_state),
        (mask_h, mask_ref),
    ]
    loads = [pltpu.make_async_copy(a, b, s_in.at[k]) for k, (a, b) in enumerate(pairs)]
    for load in loads:
        load.start()
    near_back[...] = jnp.zeros_like(near_back)
    near[...] = jnp.zeros_like(near)

    barrier = pltpu.get_barrier_semaphore()
    for peer in peers:
        pl.semaphore_signal(barrier, inc=1, device_id=(dom, peer), device_id_type=MESH)
    for distance in partners:
        pl.semaphore_signal(
            barrier, inc=1, device_id=(flipped(dom, distance), rel), device_id_type=MESH
        )

    @pl.when(has_low == 1)
    def _():
        pl.semaphore_signal(barrier, inc=1, device_id=(dom - 1, rel), device_id_type=MESH)

    @pl.when(has_high == 1)
    def _():
        pl.semaphore_signal(barrier, inc=1, device_id=(dom + 1, rel), device_id_type=MESH)

    loads[0].wait()
    table = emb_t[...]
    own_t = table.astype(bf16)
    own[...] = own_t
    low_part[...] = (table - own_t.astype(f32)).astype(bf16)
    pl.semaphore_wait(barrier, len(peers) + len(partners) + has_low + has_high)

    def remote(source, target, send, recv, device):
        return pltpu.make_async_remote_copy(
            src_ref=source,
            dst_ref=target,
            send_sem=send,
            recv_sem=recv,
            device_id=device,
            device_id_type=MESH,
        )

    def route_copy(buffer, first, step, sends, recvs, last):
        distance, _ = route[step]
        return remote(
            first if step == 0 else buffer.at[2 * step],
            last if direct else buffer.at[2 * step + 1],
            sends.at[step],
            recvs.at[step],
            (flipped(dom, distance), rel),
        )

    def routed(buffer, first, step):
        got = buffer[2 * step + 1].astype(f32)
        held = (first[...] if step == 0 else buffer[2 * step]).astype(f32)
        moved = (mask_ref[0] // (1 << route[step][1])) % 2
        return jnp.where(moved == 1, got, held)

    own_half = own.at[:, lanes(core)]
    far_half = far.at[:, lanes(core)]
    out_copy = route_copy(far_step, own_half, 0, s_route, r_route, far_half)
    out_copy.start()

    for load in loads[1:]:
        load.wait()
    bound_hot = hot(bound[...], rows)
    rim[...] = nn(own_t, bound_hot).astype(bf16)
    near_copy = remote(
        rim.at[:, lanes(core)], near.at[:, lanes(1 - core)], s_near.at[0], r_near.at[0], (beside, rel)
    )

    @pl.when(sends_near == 1)
    def _():
        near_copy.start()

    ids = jnp.concatenate(
        [jnp.full((1, tile), tile_rel[0, t], jnp.int32) for t in range(n_edge // tile)]
        + [jnp.full((1, tile), band_rel[0, t], jnp.int32) for t in range(n_band // tile)],
        axis=1,
    )
    stack = 4 * rel_count
    id_rows = lax.broadcasted_iota(jnp.int32, (stack, n_all), 0) % rel_count
    rel_hot[...] = jnp.where(id_rows == ids, 1.0, 0.0).astype(bf16)
    w = weights[...]
    w_1 = w.astype(bf16).astype(f32)
    w_2 = (w - w_1).astype(bf16).astype(f32)
    w_3 = w - w_1 - w_2
    w_stack[...] = jnp.concatenate([w_1, w_2, w_3, jnp.zeros_like(w)], axis=0).astype(bf16)
    inner = pl.ds(0, width)

    def edge_rows(at):
        hot_here = hot(src_all[:, at], rows)
        rows_here = nn(own[...], hot_here) + nn(low_part[...], hot_here)
        w_here = tn(w_stack[...], rel_hot[:, at])
        src_hot[:, at] = hot_here
        rows_t[:, at] = rows_here
        w_t[:, at] = w_here
        q_all[inner, at] = (rows_here * w_here).astype(bf16)

    over(0, n_all, edge_rows)

    def target_hot(at):
        dst_hot[:, at] = hot(dst[:, at], rows)

    over(0, n_edge, target_hot)
    if padded > width:
        rest = pl.ds(width, padded - width)
        q_all[rest, :] = jnp.zeros((padded - width, n_all), bf16)
        dt_all[rest, :] = jnp.zeros((padded - width, n_edge), bf16)
        lo_keep[rest, :] = jnp.zeros((padded - width, rows), f32)
        lo_out[rest, :] = jnp.zeros((padded - width, rows), bf16)
    bdst_hot = hot(bdst[...], rows)
    edge_ids = lax.broadcasted_iota(jnp.int32, (1, n_all), 1)
    limit = live_ref[0, 0] * tile
    valid[...] = jnp.where((edge_ids < limit) | (edge_ids >= n_edge), 1.0, 0.0)
    def edge_pos(at, target_t, weight, add):
        q_here = q_all[inner, at].astype(f32)
        pos = jnp.sum(q_here * target_t, axis=0, keepdims=True)
        dpos = -weight / (1.0 + jnp.exp(pos))
        pushed = dpos * target_t
        push[:, at] = push[:, at] + pushed if add else pushed
        return (dpos * q_here).astype(bf16)

    near_there = near.at[:, lanes(1 - core)]
    near_mate = remote(near_there, near_there, s_mate.at[0], r_mate.at[0], (dom, mate))

    @pl.when(hears_near == 1)
    def _():
        near_copy.wait_recv()
        near_mate.start()

    for step in range(len(route)):
        out_copy.wait()
        if direct:
            break
        moved = routed(far_step, own_half, step).astype(bf16)
        if step < len(route) - 1:
            far_step[2 * step + 2] = moved
            out_copy = route_copy(far_step, own_half, step + 1, s_route, r_route, far_half)
            out_copy.start()
        else:
            far_half[...] = moved
    far_copy = remote(far_half, far_half, s_far.at[0], r_far.at[0], (dom, mate))
    far_copy.start()

    @pl.when(sends_near == 1)
    def _():
        near_copy.wait_send()
        near_mate.wait_recv()

    @pl.when(hears_near == 1)
    def _():
        near_mate.wait_send()

    band_dtarget = edge_pos(
        pl.ds(n_edge, n_band), nn(near[...], bdst_hot), jnp.ones((1, n_band), f32), False
    )
    near_out[...] = nt(band_dtarget, bdst_hot).astype(bf16)
    pair_copy = remote(
        near_out.at[:, lanes(1 - core)], pair_in, s_pair.at[0], r_pair.at[0], (dom, mate)
    )
    pair_copy.start()
    def block_copy(source, target, slot, sends, recvs, peer):
        held = source.at[down(peer // 2), lanes(peer % 2)]
        return remote(held, target.at[slot], sends.at[slot], recvs.at[slot], (dom, peer))

    def same_core():
        return [(2 * k, (y + 1 + k) % n_y * 2 + core) for k in range(n_y - 1)]

    def other_core():
        others = [(2 * k + 1, (y + 1 + k) % n_y * 2 + 1 - core) for k in range(n_y - 1)]
        return others + [(2 * n_y - 2, mate)]

    def far_part(which, second):
        here = pl.ds(pl.multiple_of(which * half, half), half)
        far_rows[...] = far[:, lanes(which)].T
        row_tile = (lax.broadcasted_iota(jnp.int32, (half, 1), 0) + which * half) // tile
        counts = jnp.zeros((half, 1), f32)
        for k in range(n_neg):
            counts = counts + jnp.where(row_tile == neg_ids[0, k], 1.0, 0.0)
        scale = counts * (0.5 / (n_neg * tile))

        def edge_targets(at):
            target_t = nn(far[:, lanes(which)], dst_hot[here, at])
            dt_all[inner, at] = edge_pos(at, target_t, valid[:, at], second)

        over(0, n_edge, edge_targets)

        def edge_negs(at):
            neg = nn(far_rows[...], q_all[inner, at])
            weight = scale * valid[:, at]
            dneg[here, at] = (weight + weight * jnp.tanh(0.5 * neg)).astype(bf16)

        over(0, n_all, edge_negs)
        far_grad = nt(dt_all[...], dst_hot[here, :]) + nt(q_all[...], dneg[here, :])
        fg_out[:, lanes(which)] = far_grad.astype(bf16)
        if not second:
            fg_keep[...] = far_grad
        copies = [
            block_copy(fg_out, fg_in, slot, s_fg, r_fg, peer)
            for slot, peer in (other_core() if second else same_core())
        ]
        for copy in copies:
            copy.start()
        return copies

    fg_copies = far_part(core, False)

    pair_copy.wait()
    near_sum[...] = (near_out[:, lanes(core)].astype(f32) + pair_in[...].astype(f32)).astype(bf16)
    back_near = remote(near_sum, near_back, s_nback.at[0], r_nback.at[0], (beside, rel))

    @pl.when(sends_near == 1)
    def _():
        back_near.start()

    far_copy.wait()
    fg_copies += far_part(1 - core, True)

    def edge_sources(at):
        dq = push[:, at] + nn(far[...], dneg[:, at])
        dqw[:, at] = (dq * w_t[:, at]).astype(bf16)
        dqr[:, at] = (dq * rows_t[:, at]).astype(bf16)

    over(0, n_all, edge_sources)
    own_grad = nt(dqw[...], src_hot[...])

    @pl.when(hears_near == 1)
    def _():
        back_near.wait_recv()

    @pl.when(sends_near == 1)
    def _():
        back_near.wait_send()

    heard_hot = hot(bound[:, lanes(1 - core)], rows)
    local_grad = own_grad + nt(near_back[...], heard_hot)
    lo_keep[pl.ds(0, width), :] = local_grad
    lo_out[pl.ds(0, width), :] = local_grad.astype(bf16)
    lo_copies = [
        block_copy(lo_out, lo_in, slot, s_lo, r_lo, peer)
        for slot, peer in same_core() + other_core()
    ]
    for copy in lo_copies:
        copy.start()

    def gw_copy(level):
        return remote(
            gw_out.at[level],
            gw_in.at[level],
            s_gw.at[level],
            r_gw.at[level],
            (flipped(dom, levels[level]), rel),
        )

    def gw_step(level):
        gw_copy(level).wait()
        total = gw_out[level] + gw_in[level]
        if level < len(levels) - 1:
            gw_out[level + 1] = total
            gw_copy(level + 1).start()
        return total

    gw_out[0] = nt(rel_hot[...], dqr[...])[:rel_count]
    gw_copy(0).start()

    for copy in fg_copies:
        copy.wait()
    total = fg_keep[down(y), :]
    for k in range(n_rel - 1):
        total = total + fg_in[k].astype(f32)
    back[0] = total.astype(bf16)
    back_copy = route_copy(back, back.at[0], 0, s_back, r_back, back.at[1])
    back_copy.start()

    gw = gw_step(0)
    for copy in lo_copies:
        copy.wait()
    local = lo_keep[down(y), lanes(core)]
    for k in range(n_rel - 1):
        local = local + lo_in[k].astype(f32)

    for step in range(len(route)):
        back_copy.wait()
        if direct:
            total = back[1].astype(f32)
            break
        total = routed(back, back.at[0], step)
        if step < len(route) - 1:
            back[2 * step + 2] = total.astype(bf16)
            back_copy = route_copy(back, back.at[0], step + 1, s_back, r_back, None)
            back_copy.start()
    g_block = g_all.at[down(y), lanes(core)]
    g_block[...] = (local + total).astype(bf16)
    g_copies = [
        remote(g_block, g_block, s_g.at[k], r_g.at[k], (dom, peer))
        for k, peer in enumerate(peers)
    ]
    for copy in g_copies:
        copy.start()

    for level in range(1, len(levels)):
        gw = gw_step(level)
    eye_rel = lax.broadcasted_iota(jnp.int32, (rel_count, rel_count), 0) == (
        lax.broadcasted_iota(jnp.int32, (rel_count, rel_count), 1)
    )
    rel_col = jnp.sum(jnp.where(eye_rel, rel_state[...], 0.0), axis=1, keepdims=True)
    rel_fresh = rel_col + jnp.mean(gw * gw, axis=1, keepdims=True)
    rel_out[...] = weights[...] - step_rate * gw / jnp.sqrt(rel_fresh)

    for copy in g_copies:
        copy.wait()
    grad_t = g_all[pl.ds(0, width), :].astype(f32)
    fresh = state[...] + jnp.sum(grad_t * grad_t, axis=0, keepdims=True) * (1.0 / width)
    state_out[...] = fresh
    emb_out[...] = emb_t[...] - grad_t * (step_rate / jnp.sqrt(fresh))


def updates(n_dom, n_rel, route, collective_id, args):
    emb_t, weights = args[5], args[7]
    width, rows = emb_t.shape
    rel_count = weights.shape[0]
    n_y = n_rel // 2
    padded = pl.cdiv(width, 16 * n_y) * 16 * n_y
    part = padded // n_y
    half = rows // 2
    edges = args[9].shape[1]
    band = args[12].shape[1]
    peers = n_rel - 1
    levels = n_dom.bit_length() - 1
    steps = len(route)
    table = pltpu.VMEM((width, rows), bf16)
    side = pltpu.VMEM((width, half), bf16)
    tall = pltpu.VMEM((padded, rows), bf16)
    blocks = pltpu.VMEM((peers, part, half), bf16)
    one = pltpu.SemaphoreType.DMA((1,))
    to_peers = pltpu.SemaphoreType.DMA((peers,))
    per_step = pltpu.SemaphoreType.DMA((steps,))
    per_level = pltpu.SemaphoreType.DMA((levels,))
    small = pltpu.VMEM((levels, rel_count, width), f32)
    hbm = pl.BlockSpec(memory_space=pltpu.HBM)
    vmem = pl.BlockSpec(memory_space=pltpu.VMEM)
    semaphores = [per_step, one, one, one, one, one, to_peers, to_peers, per_step, to_peers]
    semaphores = [kind for kind in semaphores + [per_level] for _ in range(2)]
    return pl.pallas_call(
        functools.partial(kernel, n_dom, n_rel, route),
        out_shape=(
            jax.ShapeDtypeStruct((width, rows), f32),
            jax.ShapeDtypeStruct((1, rows), f32),
            jax.ShapeDtypeStruct((rel_count, width), f32),
        ),
        in_specs=[hbm] * len(args),
        out_specs=(vmem, vmem, vmem),
        scratch_shapes=[
            table,
            table,
            pltpu.VMEM((2 * steps, width, half), bf16),
            table,
            table,
            table,
            side,
            side,
            side,
            pltpu.VMEM((padded, half), f32),
            tall,
            blocks,
            pltpu.VMEM((padded, rows), f32),
            tall,
            blocks,
            pltpu.VMEM((2 * steps, part, half), bf16),
            tall,
            pltpu.VMEM((padded, edges + band), bf16),
            pltpu.VMEM((padded, edges), bf16),
            small,
            small,
            *[pltpu.SMEM(arg.shape, arg.dtype) for arg in args[:5]],
            *[pltpu.VMEM(arg.shape, arg.dtype) for arg in args[5:9]],
            pltpu.VMEM((1, edges + band), jnp.int32),
            pltpu.VMEM((1, edges), jnp.int32),
            pltpu.VMEM((1, rows), jnp.int32),
            pltpu.VMEM((1, band), jnp.int32),
            table,
            pltpu.VMEM((4 * rel_count, width), bf16),
            pltpu.VMEM((4 * rel_count, edges + band), bf16),
            pltpu.VMEM((rows, edges + band), bf16),
            pltpu.VMEM((rows, edges), bf16),
            pltpu.VMEM((width, edges + band), f32),
            pltpu.VMEM((width, edges + band), f32),
            pltpu.VMEM((width, edges + band), f32),
            pltpu.VMEM((half, width), bf16),
            pltpu.VMEM((rows, edges + band), bf16),
            pltpu.VMEM((width, edges + band), bf16),
            pltpu.VMEM((width, edges + band), bf16),
            pltpu.VMEM((1, edges + band), f32),
            pltpu.SemaphoreType.DMA((len(args),)),
        ]
        + semaphores,
        compiler_params=pltpu.CompilerParams(
            collective_id=collective_id,
            has_side_effects=True,
            vmem_limit_bytes=60 * 1024 * 1024,
        ),
    )(*args)


def body(
    emb,
    emb_state,
    rel_weight,
    rel_state,
    swap_mask,
    src_rows,
    dst_rows,
    tile_rel,
    live_tiles,
    neg_tiles,
    bound_rows,
    band_src,
    band_dst,
    band_rel,
):
    n_dom = lax.axis_size("dom")
    n_rel = lax.axis_size("rel")
    args = (
        swap_mask,
        tile_rel,
        live_tiles,
        neg_tiles,
        band_rel,
        emb.T,
        emb_state.reshape(1, -1),
        rel_weight,
        rel_state.reshape(1, -1),
        src_rows,
        dst_rows,
        bound_rows.reshape(1, -1),
        band_src,
        band_dst,
    )
    if n_dom <= 8:
        branches = [
            functools.partial(updates, n_dom, n_rel, [(m, None)], m) for m in range(1, n_dom)
        ]
        emb_t, state_new, rel_new = lax.switch(swap_mask[0] - 1, branches, args)
    else:
        route = [(1 << bit, bit) for bit in range(n_dom.bit_length() - 1)]
        emb_t, state_new, rel_new = updates(n_dom, n_rel, route, 0, args)
    return (emb_t.T, state_new.reshape(-1), rel_new)


def solution(mesh):
    in_specs = (
        P("dom", None),
        P("dom"),
        P("rel", None),
        P("rel"),
        P(),
        P("rel", "dom"),
        P("rel", "dom"),
        P("rel", "dom"),
        P("rel", "dom"),
        P("rel", "dom"),
        P("dom"),
        P("rel", "dom"),
        P("rel", "dom"),
        P("rel", "dom"),
    )
    out_specs = (P("dom", None), P("dom"), P("rel", None))
    return jax.shard_map(body, mesh=mesh, in_specs=in_specs, out_specs=out_specs, check_vma=False)
```

```python
import functools

import jax
import jax.numpy as jnp
from jax import lax
from jax.experimental import pallas as pl
from jax.experimental.pallas import tpu as pltpu
from jax.sharding import PartitionSpec as P

step_rate = 0.25
tile = 128
MESH = pl.DeviceIdType.MESH
f32 = jnp.float32
bf16 = jnp.bfloat16


def dot(a, b, dims):
    return lax.dot_general(a, b, (dims, ((), ())), preferred_element_type=f32)


def nn(a, b):
    return dot(a, b, ((1,), (0,)))


def nt(a, b):
    return dot(a, b, ((1,), (1,)))


def tn(a, b):
    return dot(a, b, ((0,), (0,)))


def flipped(index, distance):
    bit = 1
    out = index
    while bit <= distance:
        if distance & bit:
            out = out + bit * (1 - 2 * ((index // bit) % 2))
        bit *= 2
    return out


def hot(ids, count):
    rows = lax.broadcasted_iota(jnp.int32, (count, ids.shape[1]), 0)
    return jnp.where(rows == ids, 1.0, 0.0).astype(bf16)


def kernel(
    n_dom,
    n_rel,
    route,
    mask_h,
    tile_rel_h,
    live_h,
    neg_ids_h,
    band_rel_h,
    emb_h,
    state_h,
    weights_h,
    rel_state_h,
    src_h,
    dst_h,
    bound_h,
    bsrc_h,
    bdst_h,
    emb_out,
    state_out,
    rel_out,
    own,
    far,
    far_step,
    rim,
    near,
    near_out,
    pair_in,
    near_sum,
    near_back,
    fg_keep,
    fg_out,
    fg_in,
    lo_keep,
    lo_out,
    lo_in,
    back,
    g_all,
    q_all,
    dt_all,
    gw_out,
    gw_in,
    mask_ref,
    tile_rel,
    live_ref,
    neg_ids,
    band_rel,
    emb_t,
    state,
    weights,
    rel_state,
    src_all,
    dst,
    bound,
    bdst,
    low_part,
    w_stack,
    rel_hot,
    src_hot,
    dst_hot,
    rows_t,
    w_t,
    push,
    far_rows,
    dneg,
    dqw,
    dqr,
    valid,
    s_in,
    s_route,
    r_route,
    s_far,
    r_far,
    s_near,
    r_near,
    s_mate,
    r_mate,
    s_pair,
    r_pair,
    s_nback,
    r_nback,
    s_fg,
    r_fg,
    s_lo,
    r_lo,
    s_back,
    r_back,
    s_g,
    r_g,
    s_gw,
    r_gw,
):
    width, rows = emb_t.shape
    half = rows // 2
    n_y = n_rel // 2
    padded = g_all.shape[0]
    part = padded // n_y
    rel_count = weights.shape[0]
    n_edge = dst.shape[1]
    n_band = bdst.shape[1]
    n_all = n_edge + n_band
    n_neg = neg_ids.shape[1]
    dom = lax.axis_index("dom")
    rel = lax.axis_index("rel")
    y = rel // 2
    core = rel % 2
    mate = rel + 1 - 2 * core
    levels = [1 << b for b in range(n_dom.bit_length() - 1)]
    partners = sorted(set(levels) | {distance for distance, _ in route})
    direct = route[0][1] is None
    has_low = (dom + n_dom - 1) // n_dom
    has_high = 1 - dom // (n_dom - 1)
    sends_near = core * has_high + (1 - core) * has_low
    hears_near = core * has_low + (1 - core) * has_high
    beside = dom + 2 * core - 1
    peers = [lax.rem(rel + k, n_rel) for k in range(1, n_rel)]

    def lanes(which):
        return pl.ds(pl.multiple_of(which * half, half), half)

    def down(which):
        return pl.ds(pl.multiple_of(which * part, part), part)

    block = 2 * tile if n_edge % (2 * tile) == 0 and n_band % (2 * tile) == 0 else tile

    def cols(index):
        return pl.ds(pl.multiple_of(index * block, block), block)

    def over(first, last, step):
        def one(index, carry):
            step(cols(index))
            return carry

        lax.fori_loop(first // block, last // block, one, 0)

    pairs = [
        (emb_h, emb_t),
        (bound_h, bound),
        (src_h, src_all.at[:, pl.ds(0, n_edge)]),
        (bsrc_h, src_all.at[:, pl.ds(n_edge, n_band)]),
        (weights_h, weights),
        (tile_rel_h, tile_rel),
        (band_rel_h, band_rel),
        (dst_h, dst),
        (bdst_h, bdst),
        (live_h, live_ref),
        (neg_ids_h, neg_ids),
        (state_h, state),
        (rel_state_h, rel_state),
        (mask_h, mask_ref),
    ]
    loads = [pltpu.make_async_copy(a, b, s_in.at[k]) for k, (a, b) in enumerate(pairs)]
    for load in loads:
        load.start()
    near_back[...] = jnp.zeros_like(near_back)
    near[...] = jnp.zeros_like(near)

    barrier = pltpu.get_barrier_semaphore()
    for peer in peers:
        pl.semaphore_signal(barrier, inc=1, device_id=(dom, peer), device_id_type=MESH)
    for distance in partners:
        pl.semaphore_signal(
            barrier, inc=1, device_id=(flipped(dom, distance), rel), device_id_type=MESH
        )

    @pl.when(has_low == 1)
    def _():
        pl.semaphore_signal(barrier, inc=1, device_id=(dom - 1, rel), device_id_type=MESH)

    @pl.when(has_high == 1)
    def _():
        pl.semaphore_signal(barrier, inc=1, device_id=(dom + 1, rel), device_id_type=MESH)

    loads[0].wait()
    table = emb_t[...]
    own_t = table.astype(bf16)
    own[...] = own_t
    low_part[...] = (table - own_t.astype(f32)).astype(bf16)
    pl.semaphore_wait(barrier, len(peers) + len(partners) + has_low + has_high)

    def remote(source, target, send, recv, device):
        return pltpu.make_async_remote_copy(
            src_ref=source,
            dst_ref=target,
            send_sem=send,
            recv_sem=recv,
            device_id=device,
            device_id_type=MESH,
        )

    def route_copy(buffer, first, step, sends, recvs, last):
        distance, _ = route[step]
        return remote(
            first if step == 0 else buffer.at[2 * step],
            last if direct else buffer.at[2 * step + 1],
            sends.at[step],
            recvs.at[step],
            (flipped(dom, distance), rel),
        )

    def routed(buffer, first, step):
        got = buffer[2 * step + 1].astype(f32)
        held = (first[...] if step == 0 else buffer[2 * step]).astype(f32)
        moved = (mask_ref[0] // (1 << route[step][1])) % 2
        return jnp.where(moved == 1, got, held)

    own_half = own.at[:, lanes(core)]
    far_half = far.at[:, lanes(core)]
    out_copy = route_copy(far_step, own_half, 0, s_route, r_route, far_half)
    out_copy.start()

    for load in loads[1:]:
        load.wait()
    bound_hot = hot(bound[...], rows)
    rim[...] = nn(own_t, bound_hot).astype(bf16)
    near_copy = remote(
        rim.at[:, lanes(core)], near.at[:, lanes(1 - core)], s_near.at[0], r_near.at[0], (beside, rel)
    )

    @pl.when(sends_near == 1)
    def _():
        near_copy.start()

    ids = jnp.concatenate(
        [jnp.full((1, tile), tile_rel[0, t], jnp.int32) for t in range(n_edge // tile)]
        + [jnp.full((1, tile), band_rel[0, t], jnp.int32) for t in range(n_band // tile)],
        axis=1,
    )
    stack = 4 * rel_count
    id_rows = lax.broadcasted_iota(jnp.int32, (stack, n_all), 0) % rel_count
    rel_hot[...] = jnp.where(id_rows == ids, 1.0, 0.0).astype(bf16)
    w = weights[...]
    w_1 = w.astype(bf16).astype(f32)
    w_2 = (w - w_1).astype(bf16).astype(f32)
    w_3 = w - w_1 - w_2
    w_stack[...] = jnp.concatenate([w_1, w_2, w_3, jnp.zeros_like(w)], axis=0).astype(bf16)
    inner = pl.ds(0, width)

    def edge_rows(at):
        hot_here = hot(src_all[:, at], rows)
        rows_here = nn(own[...], hot_here) + nn(low_part[...], hot_here)
        w_here = tn(w_stack[...], rel_hot[:, at])
        src_hot[:, at] = hot_here
        rows_t[:, at] = rows_here
        w_t[:, at] = w_here
        q_all[inner, at] = (rows_here * w_here).astype(bf16)

    over(0, n_all, edge_rows)

    def target_hot(at):
        dst_hot[:, at] = hot(dst[:, at], rows)

    over(0, n_edge, target_hot)
    if padded > width:
        rest = pl.ds(width, padded - width)
        q_all[rest, :] = jnp.zeros((padded - width, n_all), bf16)
        dt_all[rest, :] = jnp.zeros((padded - width, n_edge), bf16)
        lo_keep[rest, :] = jnp.zeros((padded - width, rows), f32)
        lo_out[rest, :] = jnp.zeros((padded - width, rows), bf16)
    bdst_hot = hot(bdst[...], rows)
    edge_ids = lax.broadcasted_iota(jnp.int32, (1, n_all), 1)
    limit = live_ref[0, 0] * tile
    valid[...] = jnp.where((edge_ids < limit) | (edge_ids >= n_edge), 1.0, 0.0)
    row_tile = lax.broadcasted_iota(jnp.int32, (rows, 1), 0) // tile
    counts = jnp.zeros((rows, 1), f32)
    for k in range(n_neg):
        counts = counts + jnp.where(row_tile == neg_ids[0, k], 1.0, 0.0)
    scale = counts * (0.5 / (n_neg * tile))

    def edge_pos(at, target_t, weight):
        q_here = q_all[inner, at].astype(f32)
        pos = jnp.sum(q_here * target_t, axis=0, keepdims=True)
        dpos = -weight / (1.0 + jnp.exp(pos))
        push[:, at] = dpos * target_t
        return (dpos * q_here).astype(bf16)

    near_there = near.at[:, lanes(1 - core)]
    near_mate = remote(near_there, near_there, s_mate.at[0], r_mate.at[0], (dom, mate))

    @pl.when(hears_near == 1)
    def _():
        near_copy.wait_recv()
        near_mate.start()

    for step in range(len(route)):
        out_copy.wait()
        if direct:
            break
        moved = routed(far_step, own_half, step).astype(bf16)
        if step < len(route) - 1:
            far_step[2 * step + 2] = moved
            out_copy = route_copy(far_step, own_half, step + 1, s_route, r_route, far_half)
            out_copy.start()
        else:
            far_half[...] = moved
    far_copy = remote(far_half, far_half, s_far.at[0], r_far.at[0], (dom, mate))
    far_copy.start()

    @pl.when(sends_near == 1)
    def _():
        near_copy.wait_send()
        near_mate.wait_recv()

    @pl.when(hears_near == 1)
    def _():
        near_mate.wait_send()

    band_dtarget = edge_pos(
        pl.ds(n_edge, n_band), nn(near[...], bdst_hot), jnp.ones((1, n_band), f32)
    )
    near_out[...] = nt(band_dtarget, bdst_hot).astype(bf16)
    pair_copy = remote(
        near_out.at[:, lanes(1 - core)], pair_in, s_pair.at[0], r_pair.at[0], (dom, mate)
    )
    pair_copy.start()
    far_copy.wait()

    def edge_targets(at):
        dt_all[inner, at] = edge_pos(at, nn(far[...], dst_hot[:, at]), valid[:, at])

    over(0, n_edge, edge_targets)
    pair_copy.wait()
    near_sum[...] = (near_out[:, lanes(core)].astype(f32) + pair_in[...].astype(f32)).astype(bf16)
    back_near = remote(near_sum, near_back, s_nback.at[0], r_nback.at[0], (beside, rel))

    @pl.when(sends_near == 1)
    def _():
        back_near.start()

    far_rows[...] = far[...].T

    def edge_negs(at):
        neg = nn(far_rows[...], q_all[inner, at])
        weight = scale * valid[:, at]
        dneg[:, at] = (weight + weight * jnp.tanh(0.5 * neg)).astype(bf16)

    over(0, n_all, edge_negs)

    def block_copy(source, target, slot, sends, recvs, peer):
        block = source.at[down(peer // 2), lanes(peer % 2)]
        return remote(block, target.at[slot], sends.at[slot], recvs.at[slot], (dom, peer))

    def group(k):
        y_k = (y + 1 + k) % n_y
        if k == n_y - 1:
            return [(2 * k, mate)]
        return [(2 * k, y_k * 2 + core), (2 * k + 1, y_k * 2 + 1 - core)]

    fg_copies = []
    for k in range(n_y):
        band = down((y + 1 + k) % n_y)
        far_grad = nt(dt_all[band, :], dst_hot[...]) + nt(q_all[band, :], dneg[...])
        fg_out[band, :] = far_grad.astype(bf16)
        if k == n_y - 1:
            fg_keep[...] = far_grad
        for slot, peer in group(k):
            copy = block_copy(fg_out, fg_in, slot, s_fg, r_fg, peer)
            copy.start()
            fg_copies.append(copy)

    def edge_sources(at):
        dq = push[:, at] + nn(far[...], dneg[:, at])
        dqw[:, at] = (dq * w_t[:, at]).astype(bf16)
        dqr[:, at] = (dq * rows_t[:, at]).astype(bf16)

    over(0, n_all, edge_sources)
    own_grad = nt(dqw[...], src_hot[...])

    @pl.when(hears_near == 1)
    def _():
        back_near.wait_recv()

    @pl.when(sends_near == 1)
    def _():
        back_near.wait_send()

    heard_hot = hot(bound[:, lanes(1 - core)], rows)
    local_grad = own_grad + nt(near_back[...], heard_hot)
    lo_keep[pl.ds(0, width), :] = local_grad
    lo_out[pl.ds(0, width), :] = local_grad.astype(bf16)
    lo_copies = []
    for k in range(n_y):
        for slot, peer in group(k):
            copy = block_copy(lo_out, lo_in, slot, s_lo, r_lo, peer)
            copy.start()
            lo_copies.append(copy)

    def gw_copy(level):
        return remote(
            gw_out.at[level],
            gw_in.at[level],
            s_gw.at[level],
            r_gw.at[level],
            (flipped(dom, levels[level]), rel),
        )

    def gw_step(level):
        gw_copy(level).wait()
        total = gw_out[level] + gw_in[level]
        if level < len(levels) - 1:
            gw_out[level + 1] = total
            gw_copy(level + 1).start()
        return total

    gw_out[0] = nt(rel_hot[...], dqr[...])[:rel_count]
    gw_copy(0).start()

    for copy in fg_copies:
        copy.wait()
    total = fg_keep[:, lanes(core)]
    for k in range(n_rel - 1):
        total = total + fg_in[k].astype(f32)
    back[0] = total.astype(bf16)
    back_copy = route_copy(back, back.at[0], 0, s_back, r_back, back.at[1])
    back_copy.start()

    gw = gw_step(0)
    for copy in lo_copies:
        copy.wait()
    local = lo_keep[down(y), lanes(core)]
    for k in range(n_rel - 1):
        local = local + lo_in[k].astype(f32)

    for step in range(len(route)):
        back_copy.wait()
        if direct:
            total = back[1].astype(f32)
            break
        total = routed(back, back.at[0], step)
        if step < len(route) - 1:
            back[2 * step + 2] = total.astype(bf16)
            back_copy = route_copy(back, back.at[0], step + 1, s_back, r_back, None)
            back_copy.start()
    g_block = g_all.at[down(y), lanes(core)]
    g_block[...] = (local + total).astype(bf16)
    g_copies = [
        remote(g_block, g_block, s_g.at[k], r_g.at[k], (dom, peer))
        for k, peer in enumerate(peers)
    ]
    for copy in g_copies:
        copy.start()

    for level in range(1, len(levels)):
        gw = gw_step(level)
    eye_rel = lax.broadcasted_iota(jnp.int32, (rel_count, rel_count), 0) == (
        lax.broadcasted_iota(jnp.int32, (rel_count, rel_count), 1)
    )
    rel_col = jnp.sum(jnp.where(eye_rel, rel_state[...], 0.0), axis=1, keepdims=True)
    rel_fresh = rel_col + jnp.mean(gw * gw, axis=1, keepdims=True)
    rel_out[...] = weights[...] - step_rate * gw / jnp.sqrt(rel_fresh)

    for copy in g_copies:
        copy.wait()
    grad_t = g_all[pl.ds(0, width), :].astype(f32)
    fresh = state[...] + jnp.sum(grad_t * grad_t, axis=0, keepdims=True) * (1.0 / width)
    state_out[...] = fresh
    emb_out[...] = emb_t[...] - grad_t * (step_rate / jnp.sqrt(fresh))


def updates(n_dom, n_rel, route, collective_id, args):
    emb_t, weights = args[5], args[7]
    width, rows = emb_t.shape
    rel_count = weights.shape[0]
    n_y = n_rel // 2
    padded = pl.cdiv(width, 16 * n_y) * 16 * n_y
    part = padded // n_y
    half = rows // 2
    edges = args[9].shape[1]
    band = args[12].shape[1]
    peers = n_rel - 1
    levels = n_dom.bit_length() - 1
    steps = len(route)
    table = pltpu.VMEM((width, rows), bf16)
    side = pltpu.VMEM((width, half), bf16)
    tall = pltpu.VMEM((padded, rows), bf16)
    blocks = pltpu.VMEM((peers, part, half), bf16)
    one = pltpu.SemaphoreType.DMA((1,))
    to_peers = pltpu.SemaphoreType.DMA((peers,))
    per_step = pltpu.SemaphoreType.DMA((steps,))
    per_level = pltpu.SemaphoreType.DMA((levels,))
    small = pltpu.VMEM((levels, rel_count, width), f32)
    hbm = pl.BlockSpec(memory_space=pltpu.HBM)
    vmem = pl.BlockSpec(memory_space=pltpu.VMEM)
    semaphores = [per_step, one, one, one, one, one, to_peers, to_peers, per_step, to_peers]
    semaphores = [kind for kind in semaphores + [per_level] for _ in range(2)]
    return pl.pallas_call(
        functools.partial(kernel, n_dom, n_rel, route),
        out_shape=(
            jax.ShapeDtypeStruct((width, rows), f32),
            jax.ShapeDtypeStruct((1, rows), f32),
            jax.ShapeDtypeStruct((rel_count, width), f32),
        ),
        in_specs=[hbm] * len(args),
        out_specs=(vmem, vmem, vmem),
        scratch_shapes=[
            table,
            table,
            pltpu.VMEM((2 * steps, width, half), bf16),
            table,
            table,
            table,
            side,
            side,
            side,
            pltpu.VMEM((part, rows), f32),
            tall,
            blocks,
            pltpu.VMEM((padded, rows), f32),
            tall,
            blocks,
            pltpu.VMEM((2 * steps, part, half), bf16),
            tall,
            pltpu.VMEM((padded, edges + band), bf16),
            pltpu.VMEM((padded, edges), bf16),
            small,
            small,
            *[pltpu.SMEM(arg.shape, arg.dtype) for arg in args[:5]],
            *[pltpu.VMEM(arg.shape, arg.dtype) for arg in args[5:9]],
            pltpu.VMEM((1, edges + band), jnp.int32),
            pltpu.VMEM((1, edges), jnp.int32),
            pltpu.VMEM((1, rows), jnp.int32),
            pltpu.VMEM((1, band), jnp.int32),
            table,
            pltpu.VMEM((4 * rel_count, width), bf16),
            pltpu.VMEM((4 * rel_count, edges + band), bf16),
            pltpu.VMEM((rows, edges + band), bf16),
            pltpu.VMEM((rows, edges), bf16),
            pltpu.VMEM((width, edges + band), f32),
            pltpu.VMEM((width, edges + band), f32),
            pltpu.VMEM((width, edges + band), f32),
            pltpu.VMEM((rows, width), bf16),
            pltpu.VMEM((rows, edges + band), bf16),
            pltpu.VMEM((width, edges + band), bf16),
            pltpu.VMEM((width, edges + band), bf16),
            pltpu.VMEM((1, edges + band), f32),
            pltpu.SemaphoreType.DMA((len(args),)),
        ]
        + semaphores,
        compiler_params=pltpu.CompilerParams(
            collective_id=collective_id,
            has_side_effects=True,
            vmem_limit_bytes=64 * 1024 * 1024,
        ),
    )(*args)


def body(
    emb,
    emb_state,
    rel_weight,
    rel_state,
    swap_mask,
    src_rows,
    dst_rows,
    tile_rel,
    live_tiles,
    neg_tiles,
    bound_rows,
    band_src,
    band_dst,
    band_rel,
):
    n_dom = lax.axis_size("dom")
    n_rel = lax.axis_size("rel")
    args = (
        swap_mask,
        tile_rel,
        live_tiles,
        neg_tiles,
        band_rel,
        emb.T,
        emb_state.reshape(1, -1),
        rel_weight,
        rel_state.reshape(1, -1),
        src_rows,
        dst_rows,
        bound_rows.reshape(1, -1),
        band_src,
        band_dst,
    )
    if n_dom <= 8:
        branches = [
            functools.partial(updates, n_dom, n_rel, [(m, None)], m) for m in range(1, n_dom)
        ]
        emb_t, state_new, rel_new = lax.switch(swap_mask[0] - 1, branches, args)
    else:
        route = [(1 << bit, bit) for bit in range(n_dom.bit_length() - 1)]
        emb_t, state_new, rel_new = updates(n_dom, n_rel, route, 0, args)
    return (emb_t.T, state_new.reshape(-1), rel_new)


def solution(mesh):
    in_specs = (
        P("dom", None),
        P("dom"),
        P("rel", None),
        P("rel"),
        P(),
        P("rel", "dom"),
        P("rel", "dom"),
        P("rel", "dom"),
        P("rel", "dom"),
        P("rel", "dom"),
        P("dom"),
        P("rel", "dom"),
        P("rel", "dom"),
        P("rel", "dom"),
    )
    out_specs = (P("dom", None), P("dom"), P("rel", None))
    return jax.shard_map(body, mesh=mesh, in_specs=in_specs, out_specs=out_specs, check_vma=False)
```
